768 devices in a mesh: blk: 192 (over y, z, x_lo), col: 4 (over x_hi, core).
Axes of the slice: x: 4 (x_hi: 2, x_lo: 2; x = x_hi * 2 + x_lo), y: 8, z: 12, core: 2. Of those that a mesh axis runs over, the one named last changes fastest.
Arguments:
- node_feats: bfloat16 [98304, 512], P('blk', 'col'), may hold values from -6 to 6
- weight: bfloat16 [512, 512], replicated, may hold values from -0.25 to 0.25
- layer_bias: bfloat16 [512], P('col'), may hold values from -4 to 4
- cotangent: bfloat16 [98304, 512], P('blk', 'col'), may hold values from -6 to 6
- adj_tiles: bfloat16 [192, 9, 16, 128, 128], P('blk'), may hold values from -0.1796875 to 0.1796875
- tile_row: int32 [192, 9, 16], P('blk'), may hold values from 0 to 3, as said below
- tile_col: int32 [192, 9, 16], P('blk'), may hold values from 0 to 3
- tile_count: int32 [192, 9], P('blk'), may hold values from 1 to 16, as said below
Outputs:
- activated: bfloat16 [98304, 512], P('blk', 'col')
- grad_nodes: bfloat16 [98304, 512], P('blk', 'col')
- grad_weight: float32 [512, 512], P(None, 'col')
- grad_bias: float32 [512], P('col')
The draws below stay inside these ranges and needn't reach their ends.
Inputs may be any that keep to these rules, and one draw needn't show every extreme that they name: Within one device and offset, the 16 slots (live or not) name distinct pairs of tile_row and tile_col. `tile_count`: some device and offset has all 16 slots live in every draw.
All inputs are finite; a program needn't handle non-finite values.
Results may differ from the reference program's by a relative error of at most 0.0095.
Values may be sent and summed in bfloat16 or wider, within the bound.
No kernel may reach another device: no remote copies, remote signals or barrier semaphores. Data moves between devices by JAX's collectives and lax.ppermute only.
A program may use at most 32 MiB of HBM per device.

```python
import jax
import jax.numpy as jnp
from jax import lax

HIDDEN_SIZE = 512
TILE_SIZE = 128
ROW_BLOCKS = 4
CAPACITY = 16
REACH_DEVS = 4
OFFSETS = 9
NODES = 98304
N_BLK = 192


def tile_slots(key):
    pairs = ROW_BLOCKS * ROW_BLOCKS
    scores = jax.random.randint(key, (N_BLK, OFFSETS, pairs), 0, 1 << 20)
    scores = scores * pairs + jnp.arange(pairs, dtype=jnp.int32)
    order = jnp.argsort(scores, axis=-1, stable=True)[..., :CAPACITY]
    return order.astype(jnp.int32)


def draw_tile_row(key, part):
    chosen = tile_slots(key)
    return (chosen // ROW_BLOCKS).astype(jnp.int32)


def draw_tile_col(key, part):
    chosen = tile_slots(key)
    return (chosen % ROW_BLOCKS).astype(jnp.int32)


def draw_tile_count(key, part):
    key = jax.random.fold_in(key, 3)
    first, second, third, fourth = jax.random.split(key, 4)
    base_count = jax.random.randint(first, (N_BLK, OFFSETS), 1, CAPACITY // 4 + 1)
    factor = jax.random.randint(second, (N_BLK, 1), 1, 5)
    counts = base_count * factor
    device = jax.random.randint(third, (), 0, N_BLK)
    offset = jax.random.randint(fourth, (), 0, OFFSETS)
    counts = counts.at[device, offset].set(CAPACITY)
    return counts.astype(jnp.int32)


def level_of(rng, shape, cuts, low, largest):
    def one(dim, shards_of):
        steps = jax.random.uniform(jax.random.fold_in(jax.random.fold_in(rng, 6), dim), (shards_of,), jnp.float32, low / len(cuts), largest / len(cuts))
        return jnp.repeat(jnp.exp(steps), shape[dim] // shards_of).reshape((-1,) + (1,) * (len(shape) - dim - 1))

    factor_of = one(*cuts[0])
    for cut in cuts[1:]:
        factor_of = factor_of * one(*cut)
    return factor_of


def normal_values(key, extent, scale, most, pieces=(), held_as=jnp.bfloat16):
    array = scale * jax.random.normal(key, extent, jnp.float32)
    if pieces:
        array = array * level_of(key, extent, pieces, -0.22, 0.18)
    return jnp.clip(array, -most, most).astype(held_as)


def setup_inputs(seed: int = 0) -> dict:
    seeds = jax.random.split(jax.random.key(seed), 9)
    node_feats = normal_values(seeds[0], (NODES, HIDDEN_SIZE), 1.0, 6.0, ((0, 192), (1, 4)))
    weight = normal_values(seeds[1], (HIDDEN_SIZE, HIDDEN_SIZE), HIDDEN_SIZE ** -0.5, 0.25)
    layer_bias = normal_values(seeds[2], (HIDDEN_SIZE,), 1.0, 4.0, ((0, 4),))
    cotangent = normal_values(seeds[3], (NODES, HIDDEN_SIZE), 1.0, 6.0, ((0, 192), (1, 4)))
    adj_tiles = normal_values(seeds[4], (N_BLK, OFFSETS, CAPACITY, TILE_SIZE, TILE_SIZE), 0.03, 0.1796875, ((0, 192),))
    tile_row = draw_tile_row(jax.random.fold_in(seeds[8], 71), 0)
    tile_col = draw_tile_col(jax.random.fold_in(seeds[8], 71), 0)
    tile_count = draw_tile_count(jax.random.fold_in(seeds[8], 71), 0)
    return {"node_feats": node_feats, "weight": weight, "layer_bias": layer_bias, "cotangent": cotangent, "adj_tiles": adj_tiles, "tile_row": tile_row, "tile_col": tile_col, "tile_count": tile_count}


def reference(node_feats, weight, layer_bias, cotangent, adj_tiles, tile_row, tile_col, tile_count):
    projected = jnp.dot(node_feats, weight, preferred_element_type=jnp.float32).astype(jnp.bfloat16)
    proj_blocks = projected.reshape(N_BLK, ROW_BLOCKS, TILE_SIZE, HIDDEN_SIZE)
    slot_ids = jnp.arange(CAPACITY, dtype=jnp.int32)
    block_ids = jnp.arange(ROW_BLOCKS, dtype=jnp.int32)
    offset_ids = jnp.arange(OFFSETS, dtype=jnp.int32)

    def forward_device(device):

        def per_offset(summed, offset):
            source = (device + offset - REACH_DEVS) % N_BLK
            picked = jnp.take(proj_blocks[source], tile_col[device, offset], axis=0)
            products = jnp.einsum('kab,kbh->kah', adj_tiles[device, offset].astype(jnp.float32), picked.astype(jnp.float32))
            live_slots = slot_ids < tile_count[device, offset]
            placing = ((tile_row[device, offset][None, :] == block_ids[:, None]) & live_slots[None, :]).astype(jnp.float32)
            added = jnp.einsum('rk,kah->rah', placing, products, precision=lax.Precision.HIGHEST)
            return (summed + added, None)
        start = jnp.zeros((ROW_BLOCKS, TILE_SIZE, HIDDEN_SIZE), jnp.float32)
        summed, unused = lax.scan(per_offset, start, offset_ids)
        return summed
    aggregated = lax.map(forward_device, jnp.arange(N_BLK, dtype=jnp.int32)).reshape(NODES, HIDDEN_SIZE)
    preact = aggregated + layer_bias.astype(jnp.float32)[None, :]
    sigmoid_val = jax.nn.sigmoid(preact)
    activated = (preact * sigmoid_val).astype(jnp.bfloat16)
    grad_pre = (cotangent.astype(jnp.float32) * sigmoid_val * (1.0 + preact * (1.0 - sigmoid_val))).astype(jnp.bfloat16)
    pre_blocks = grad_pre.reshape(N_BLK, ROW_BLOCKS, TILE_SIZE, HIDDEN_SIZE)

    def backward_device(target):

        def per_offset(summed, offset):
            owner = (target - (offset - REACH_DEVS)) % N_BLK
            picked = jnp.take(pre_blocks[owner], tile_row[owner, offset], axis=0)
            products = jnp.einsum('kba,kbh->kah', adj_tiles[owner, offset].astype(jnp.float32), picked.astype(jnp.float32))
            live_slots = slot_ids < tile_count[owner, offset]
            placing = ((tile_col[owner, offset][None, :] == block_ids[:, None]) & live_slots[None, :]).astype(jnp.float32)
            added = jnp.einsum('rk,kah->rah', placing, products, precision=lax.Precision.HIGHEST)
            rounded = lax.optimization_barrier(added.astype(jnp.bfloat16))
            return (summed + rounded.astype(jnp.float32), None)
        start = jnp.zeros((ROW_BLOCKS, TILE_SIZE, HIDDEN_SIZE), jnp.float32)
        summed, unused = lax.scan(per_offset, start, offset_ids)
        return summed
    grad_proj = lax.map(backward_device, jnp.arange(N_BLK, dtype=jnp.int32)).reshape(NODES, HIDDEN_SIZE).astype(jnp.bfloat16)
    grad_scale = 1.0 / jnp.sqrt(jnp.float32(NODES))
    grad_weight = lax.dot_general(node_feats, grad_proj, (((0,), (0,)), ((), ())), preferred_element_type=jnp.float32) * grad_scale
    grad_bias = lax.optimization_barrier(jnp.sum(grad_pre.astype(jnp.float32), axis=0)) * grad_scale
    grad_nodes = lax.dot_general(grad_proj, weight, (((1,), (1,)), ((), ())), preferred_element_type=jnp.float32).astype(jnp.bfloat16)
    return (activated, grad_nodes, grad_weight, grad_bias)
```

```python
import jax
import jax.numpy as jnp
import numpy as np
from jax import lax
from jax.experimental import pallas as pl
from jax.experimental.pallas import tpu as pltpu
from jax.sharding import Mesh
from jax.sharding import PartitionSpec as P

NODES = 98304
TILE = 128
BLOCKS = 4
ROWS = TILE * BLOCKS
WIDTH = 128
COLS = 4
HIDDEN = WIDTH * COLS
OFFSETS = 9
SLOTS = 16
REACH = 4
WINDOW = OFFSETS + 1
N_Y, N_Z, N_XL = 8, 12, 2
PAIRS = N_Y * N_Z
PACK_ROWS = ROWS + 16
RING = N_Z * N_XL
SHARE = 24
BLK = ("y", "z", "xl")
COL = ("xh", "core")
BF16 = jnp.bfloat16
F32 = jnp.float32
VMEM = pl.BlockSpec(memory_space=pltpu.VMEM)
SMEM = pl.BlockSpec(memory_space=pltpu.SMEM)


def params(**more):
    return pltpu.CompilerParams(vmem_limit_bytes=32 * 1024 * 1024, **more)


def dense_kernel(side, rows, cols, counts, slab, dense):
    place = pl.program_id(0)
    offset = place - side[0]
    inside = (offset >= 0) & (offset < OFFSETS)

    @pl.when(inside)
    def _():
        live = counts[offset]
        for slot in range(SLOTS):
            at = offset * SLOTS + slot
            row = pl.multiple_of(rows[at] * TILE, TILE)
            col = pl.multiple_of(cols[at] * TILE, TILE)
            tile = slab[0, slot]
            dense[0, pl.ds(row, TILE), pl.ds(col, TILE)] = jnp.where(
                slot < live, tile, jnp.zeros_like(tile)
            )

    @pl.when(jnp.logical_not(inside))
    def _():
        dense[...] = jnp.zeros_like(dense)


def make_dense(side, rows, cols, counts, slab):
    return pl.pallas_call(
        dense_kernel,
        grid_spec=pltpu.PrefetchScalarGridSpec(
            num_scalar_prefetch=4,
            grid=(WINDOW,),
            in_specs=[
                pl.BlockSpec(
                    (1, SLOTS, TILE, TILE),
                    lambda j, side, *_: (jnp.clip(j - side[0], 0, OFFSETS - 1), 0, 0, 0),
                )
            ],
            out_specs=pl.BlockSpec((1, ROWS, ROWS), lambda j, *_: (j, 0, 0)),
        ),
        out_shape=jax.ShapeDtypeStruct((WINDOW, ROWS, ROWS), BF16),
        compiler_params=params(),
        cost_estimate=pl.CostEstimate(flops=0, bytes_accessed=10 << 20, transcendentals=0),
        name="dense_tiles",
    )(side, rows, cols, counts, slab)


def gather_kernel(dense, xa, xb, xc, xd, xe, out):
    total = jnp.zeros((ROWS, WIDTH), F32)
    for k, pair in enumerate((xa, xb, xc, xd, xe)):
        for s in range(2):
            total += jnp.dot(dense[2 * k + s], pair[s], preferred_element_type=F32)
    out[...] = total.astype(BF16)


def gather_rows(dense, pairs):
    return pl.pallas_call(
        gather_kernel,
        in_specs=[VMEM] * 6,
        out_specs=VMEM,
        out_shape=jax.ShapeDtypeStruct((ROWS, WIDTH), BF16),
        compiler_params=params(),
        cost_estimate=pl.CostEstimate(
            flops=2 * WINDOW * ROWS * ROWS * WIDTH, bytes_accessed=8 << 20, transcendentals=0
        ),
        name="aggregate_features",
    )(dense, *pairs)


def middle_kernel(column, mixed, packed, weight, dense, act, part, ta, tb, tc, td, te, act_all, grad_all, feats):
    mine = pl.multiple_of(column[0] * WIDTH, WIDTH)
    bias = jnp.concatenate(
        [packed[c, ROWS:, :] for c in range(COLS)], axis=1
    )[0:1].astype(F32)
    step = 128
    for i in range(ROWS // step):
        span = slice(i * step, (i + 1) * step)
        own = jnp.concatenate([mixed[c, span, :] for c in range(COLS)], axis=1)
        feats[span, :] = own
        preact = jnp.dot(own, weight[...], preferred_element_type=F32) + bias
        sig = 1.0 / (1.0 + jnp.exp(-preact))
        act_all[span, :] = (preact * sig).astype(BF16)
        cot = jnp.concatenate([packed[c, span, :] for c in range(COLS)], axis=1)
        grad_all[span, :] = (
            cot.astype(F32) * sig * (1.0 + preact * (1.0 - sig))
        ).astype(BF16)
    act[...] = act_all[:, pl.ds(mine, WIDTH)]
    grad_mine = grad_all[:, pl.ds(mine, WIDTH)].astype(F32)
    weight_grad = jnp.dot(
        grad_mine.T.astype(BF16), feats[...], preferred_element_type=F32
    )
    part[0:ROWS, :] = weight_grad.T
    first = lax.broadcasted_iota(jnp.int32, (RING * SHARE - HIDDEN, WIDTH), 0) == 0
    part[ROWS:, :] = jnp.where(first, jnp.sum(grad_mine, axis=0, keepdims=True), 0.0)
    back = lax.dot_general(
        weight[pl.ds(mine, WIDTH), :],
        grad_all[...],
        (((1,), (1,)), ((), ())),
        preferred_element_type=F32,
    ).astype(BF16)
    for k, pair in enumerate((ta, tb, tc, td, te)):
        for s in range(2):
            pair[s] = jnp.dot(back, dense[2 * k + s], preferred_element_type=F32).astype(BF16)


def middle(column, mixed, packed, weight, dense):
    term = jax.ShapeDtypeStruct((2, WIDTH, ROWS), BF16)
    return pl.pallas_call(
        middle_kernel,
        in_specs=[SMEM] + [VMEM] * 4,
        out_specs=[VMEM] * 7,
        out_shape=[
            jax.ShapeDtypeStruct((ROWS, WIDTH), BF16),
            jax.ShapeDtypeStruct((RING * SHARE, WIDTH), F32),
        ]
        + [term] * 5,
        scratch_shapes=[pltpu.VMEM((ROWS, HIDDEN), BF16)] * 3,
        compiler_params=params(),
        cost_estimate=pl.CostEstimate(
            flops=2 * (WINDOW + 9) * ROWS * ROWS * WIDTH, bytes_accessed=10 << 20, transcendentals=ROWS * HIDDEN
        ),
        name="activation_and_terms",
    )(column, mixed, packed, weight, dense)


def split_kernel(side, own, ta, tb, td, te, keep, send):
    for s in range(2):
        total = own[s].astype(F32)
        for arrived in (ta, tb, td, te):
            total += arrived[s].astype(F32)

        @pl.when(side[0] == s)
        def _():
            keep[...] = total

        @pl.when(side[0] != s)
        def _():
            send[...] = total.astype(BF16)


def split_terms(side, own, arrived):
    return pl.pallas_call(
        split_kernel,
        in_specs=[SMEM] + [VMEM] * 5,
        out_specs=[VMEM] * 2,
        out_shape=[
            jax.ShapeDtypeStruct((WIDTH, ROWS), F32),
            jax.ShapeDtypeStruct((WIDTH, ROWS), BF16),
        ],
        compiler_params=params(),
        cost_estimate=pl.CostEstimate(flops=1 << 20, bytes_accessed=2 << 20, transcendentals=0),
        name="pair_sums",
    )(side, own, *arrived)


def last_kernel(keep, arrived, out):
    out[...] = (keep[...] + arrived[...].astype(F32)).T.astype(BF16)


def last_sum(keep, arrived):
    return pl.pallas_call(
        last_kernel,
        in_specs=[VMEM] * 2,
        out_specs=VMEM,
        out_shape=jax.ShapeDtypeStruct((ROWS, WIDTH), BF16),
        compiler_params=params(),
        cost_estimate=pl.CostEstimate(flops=1 << 17, bytes_accessed=1 << 19, transcendentals=0),
        name="node_gradient",
    )(keep, arrived)


def from_pair(block, hops):
    route = [
        (2 * ((p + hops) % PAIRS) + s, 2 * p + s) for p in range(PAIRS) for s in range(2)
    ]
    return lax.ppermute(block, BLK, route)


def on_device(node_feats, weight, layer_bias, cotangent, adj_tiles, tile_row, tile_col, tile_count):
    side = lax.axis_index("xl").astype(jnp.int32).reshape(1)
    column = lax.axis_index(COL).astype(jnp.int32).reshape(1)

    dense = make_dense(
        side, tile_row.reshape(-1), tile_col.reshape(-1), tile_count.reshape(-1), adj_tiles[0]
    )
    with jax.named_scope("feature_halo"):
        pair = lax.all_gather(node_feats, "xl", axis=0, tiled=False)
        pairs = [pair if k == 0 else from_pair(pair, k) for k in (-2, -1, 0, 1, 2)]
    mine = gather_rows(dense, pairs)
    with jax.named_scope("column_gather"):
        packed = jnp.concatenate([cotangent, jnp.broadcast_to(layer_bias[None], (16, WIDTH))], axis=0)
        packed = lax.all_gather(packed, COL, axis=0, tiled=False)
        mixed = lax.all_gather(mine, COL, axis=0, tiled=False)
    act, part, ta, tb, tc, td, te = middle(column, mixed, packed, weight, dense)

    with jax.named_scope("term_halo"):
        arrived = [from_pair(t, -k) for k, t in ((-2, ta), (-1, tb), (1, td), (2, te))]
    keep, send = split_terms(side, tc, arrived)
    with jax.named_scope("term_exchange"):
        swap = [(b ^ 1, b) for b in range(2 * PAIRS)]
        other = lax.ppermute(send, BLK, swap)
    grad_nodes = last_sum(keep, other)

    with jax.named_scope("weight_sum"):
        ring = ("z", "xl")
        shares = lax.all_to_all(part.reshape(RING, SHARE, WIDTH), ring, 0, 0, tiled=True)
        share = jnp.sum(shares, axis=0)
        shares = lax.all_to_all(
            jnp.broadcast_to(share[None], (N_Y, SHARE, WIDTH)), "y", 0, 0, tiled=True
        )
        share = jnp.sum(shares, axis=0) * (1.0 / jnp.sqrt(F32(NODES)))
        whole = lax.all_to_all(
            jnp.broadcast_to(share[None], (RING, SHARE, WIDTH)), ring, 0, 0, tiled=True
        ).reshape(RING * SHARE, WIDTH)
    return act, grad_nodes, whole[:HIDDEN], whole[HIDDEN]


def solution(mesh):
    fine = Mesh(
        np.asarray(mesh.devices).reshape(N_Y, N_Z, N_XL, 2, 2), ("y", "z", "xl", "xh", "core")
    )
    placed = (
        P(BLK, COL),
        P(),
        P(COL),
        P(BLK, COL),
        P(BLK, None, None, None, None),
        P(BLK, None, None),
        P(BLK, None, None),
        P(BLK, None),
    )
    return jax.shard_map(
        on_device,
        mesh=fine,
        in_specs=placed,
        out_specs=(P(BLK, COL), P(BLK, COL), P(None, COL), P(COL)),
        check_vma=False,
    )
```

```python
import jax
import jax.numpy as jnp
import numpy as np
from jax import lax
from jax.experimental import pallas as pl
from jax.experimental.pallas import tpu as pltpu
from jax.sharding import Mesh
from jax.sharding import PartitionSpec as P

NODES = 98304
TILE = 128
BLOCKS = 4
ROWS = TILE * BLOCKS
WIDTH = 128
COLS = 4
HIDDEN = WIDTH * COLS
OFFSETS = 9
SLOTS = 16
REACH = 4
WINDOW = OFFSETS + 1
N_Y, N_Z, N_XL = 8, 12, 2
PAIRS = N_Y * N_Z
PACK_ROWS = ROWS + 16
RING = N_Z * N_XL
SHARE = 24
BLK = ("y", "z", "xl")
COL = ("xh", "core")
BF16 = jnp.bfloat16
F32 = jnp.float32
VMEM = pl.BlockSpec(memory_space=pltpu.VMEM)
SMEM = pl.BlockSpec(memory_space=pltpu.SMEM)


def params(mib=32):
    return pltpu.CompilerParams(vmem_limit_bytes=mib * 1024 * 1024)


def dense_kernel(side, rows, cols, counts, slab, dense):
    place = pl.program_id(0)
    offset = place - side[0]
    inside = (offset >= 0) & (offset < OFFSETS)

    @pl.when(inside)
    def _():
        live = counts[0, offset]
        for slot in range(SLOTS):
            row = pl.multiple_of(rows[0, offset, slot] * TILE, TILE)
            col = pl.multiple_of(cols[0, offset, slot] * TILE, TILE)
            tile = slab[0, 0, slot]
            dense[0, pl.ds(row, TILE), pl.ds(col, TILE)] = jnp.where(
                slot < live, tile, jnp.zeros_like(tile)
            )

    @pl.when(jnp.logical_not(inside))
    def _():
        dense[...] = jnp.zeros_like(dense)


def make_dense(side, rows, cols, counts, slab):
    return pl.pallas_call(
        dense_kernel,
        grid_spec=pltpu.PrefetchScalarGridSpec(
            num_scalar_prefetch=4,
            grid=(WINDOW,),
            in_specs=[
                pl.BlockSpec(
                    (1, 1, SLOTS, TILE, TILE),
                    lambda j, side, *_: (0, jnp.clip(j - side[0], 0, OFFSETS - 1), 0, 0, 0),
                )
            ],
            out_specs=pl.BlockSpec((1, ROWS, ROWS), lambda j, *_: (j, 0, 0)),
        ),
        out_shape=jax.ShapeDtypeStruct((WINDOW, ROWS, ROWS), BF16),
        compiler_params=params(),
        cost_estimate=pl.CostEstimate(flops=0, bytes_accessed=10 << 20, transcendentals=0),
        name="dense_tiles",
    )(side, rows, cols, counts, slab)


def gather_kernel(dense, xa, xb, xc, xd, xe, out):
    total = jnp.zeros((ROWS, WIDTH), F32)
    for k, pair in enumerate((xa, xb, xc, xd, xe)):
        for s in range(2):
            total += jnp.dot(dense[2 * k + s], pair[s], preferred_element_type=F32)
    out[...] = total.astype(BF16)


def gather_rows(dense, pairs):
    return pl.pallas_call(
        gather_kernel,
        in_specs=[VMEM] * 6,
        out_specs=VMEM,
        out_shape=jax.ShapeDtypeStruct((ROWS, WIDTH), BF16),
        compiler_params=params(),
        cost_estimate=pl.CostEstimate(
            flops=2 * WINDOW * ROWS * ROWS * WIDTH, bytes_accessed=8 << 20, transcendentals=0
        ),
        name="aggregate_features",
    )(dense, *pairs)


def middle_kernel(column, mixed, packed, weight, dense, act, part, ta, tb, tc, td, te, act_all, grad_all, feats):
    mine = pl.multiple_of(column[0] * WIDTH, WIDTH)
    bias = jnp.concatenate(
        [packed[c, ROWS:, :] for c in range(COLS)], axis=1
    )[0:1].astype(F32)
    step = 128
    for i in range(ROWS // step):
        span = slice(i * step, (i + 1) * step)
        own = jnp.concatenate([mixed[c, span, :] for c in range(COLS)], axis=1)
        feats[span, :] = own
        preact = jnp.dot(own, weight[...], preferred_element_type=F32) + bias
        sig = 1.0 / (1.0 + jnp.exp(-preact))
        act_all[span, :] = (preact * sig).astype(BF16)
        cot = jnp.concatenate([packed[c, span, :] for c in range(COLS)], axis=1)
        grad_all[span, :] = (
            cot.astype(F32) * sig * (1.0 + preact * (1.0 - sig))
        ).astype(BF16)
    act[...] = act_all[:, pl.ds(mine, WIDTH)]
    grad_mine = grad_all[:, pl.ds(mine, WIDTH)].astype(F32)
    weight_grad = jnp.dot(
        grad_mine.T.astype(BF16), feats[...], preferred_element_type=F32
    )
    part[0:ROWS, :] = weight_grad.T
    first = lax.broadcasted_iota(jnp.int32, (RING * SHARE - HIDDEN, WIDTH), 0) == 0
    part[ROWS:, :] = jnp.where(first, jnp.sum(grad_mine, axis=0, keepdims=True), 0.0)
    back = lax.dot_general(
        weight[pl.ds(mine, WIDTH), :],
        grad_all[...],
        (((1,), (1,)), ((), ())),
        preferred_element_type=F32,
    ).astype(BF16)
    for k, pair in enumerate((ta, tb, tc, td, te)):
        for s in range(2):
            pair[s] = jnp.dot(back, dense[2 * k + s], preferred_element_type=F32).astype(BF16)


def middle(column, mixed, packed, weight, dense):
    term = jax.ShapeDtypeStruct((2, WIDTH, ROWS), BF16)
    return pl.pallas_call(
        middle_kernel,
        in_specs=[SMEM] + [VMEM] * 4,
        out_specs=[VMEM] * 7,
        out_shape=[
            jax.ShapeDtypeStruct((ROWS, WIDTH), BF16),
            jax.ShapeDtypeStruct((RING * SHARE, WIDTH), F32),
        ]
        + [term] * 5,
        scratch_shapes=[pltpu.VMEM((ROWS, HIDDEN), BF16)] * 3,
        compiler_params=params(),
        cost_estimate=pl.CostEstimate(
            flops=2 * (WINDOW + 9) * ROWS * ROWS * WIDTH, bytes_accessed=10 << 20, transcendentals=ROWS * HIDDEN
        ),
        name="activation_and_terms",
    )(column, mixed, packed, weight, dense)


def split_kernel(side, own, ta, tb, td, te, shares, keep, send, spread):
    for s in range(2):
        total = own[s].astype(F32)
        for arrived in (ta, tb, td, te):
            total += arrived[s].astype(F32)

        @pl.when(side[0] == s)
        def _():
            keep[...] = total

        @pl.when(side[0] != s)
        def _():
            send[...] = total.astype(BF16)

    spread[...] = jnp.broadcast_to(jnp.sum(shares[...], axis=0)[None], spread.shape)


def split_terms(side, own, arrived, shares):
    return pl.pallas_call(
        split_kernel,
        in_specs=[SMEM] + [VMEM] * 6,
        out_specs=[VMEM] * 3,
        out_shape=[
            jax.ShapeDtypeStruct((WIDTH, ROWS), F32),
            jax.ShapeDtypeStruct((WIDTH, ROWS), BF16),
            jax.ShapeDtypeStruct((N_Y, SHARE, WIDTH), F32),
        ],
        compiler_params=params(),
        cost_estimate=pl.CostEstimate(flops=1 << 20, bytes_accessed=2 << 20, transcendentals=0),
        name="pair_sums",
    )(side, own, *arrived, shares)


def last_kernel(keep, arrived, shares, out, spread):
    out[...] = (keep[...] + arrived[...].astype(F32)).T.astype(BF16)
    total = jnp.sum(shares[...], axis=0) * (1.0 / jnp.sqrt(F32(NODES)))
    spread[...] = jnp.broadcast_to(total.astype(BF16)[None], spread.shape)


def last_sum(keep, arrived, shares):
    return pl.pallas_call(
        last_kernel,
        in_specs=[VMEM] * 3,
        out_specs=[VMEM] * 2,
        out_shape=[
            jax.ShapeDtypeStruct((ROWS, WIDTH), BF16),
            jax.ShapeDtypeStruct((RING, SHARE, WIDTH), BF16),
        ],
        compiler_params=params(),
        cost_estimate=pl.CostEstimate(flops=1 << 17, bytes_accessed=1 << 19, transcendentals=0),
        name="node_gradient",
    )(keep, arrived, shares)


def from_pair(block, hops):
    route = [
        (2 * ((p + hops) % PAIRS) + s, 2 * p + s) for p in range(PAIRS) for s in range(2)
    ]
    return lax.ppermute(block, BLK, route)


def on_device(node_feats, weight, layer_bias, cotangent, adj_tiles, tile_row, tile_col, tile_count):
    side = lax.axis_index("xl").astype(jnp.int32).reshape(1)
    column = lax.axis_index(COL).astype(jnp.int32).reshape(1)

    dense = make_dense(side, tile_row, tile_col, tile_count, adj_tiles)
    with jax.named_scope("feature_halo"):
        pair = lax.all_gather(node_feats, "xl", axis=0, tiled=False)
        pairs = [pair if k == 0 else from_pair(pair, k) for k in (-2, -1, 0, 1, 2)]
    mine = gather_rows(dense, pairs)
    with jax.named_scope("column_gather"):
        packed = jnp.concatenate([cotangent, jnp.broadcast_to(layer_bias[None], (16, WIDTH))], axis=0)
        packed = jnp.broadcast_to(packed[None], (COLS, PACK_ROWS, WIDTH))
        packed = lax.all_to_all(packed, COL, 0, 0, tiled=True)
        mixed = lax.all_gather(mine, COL, axis=0, tiled=False)
    act, part, ta, tb, tc, td, te = middle(column, mixed, packed, weight, dense)

    ring = ("z", "xl")
    with jax.named_scope("weight_scatter"):
        shares = lax.all_to_all(part.reshape(RING, SHARE, WIDTH), ring, 0, 0, tiled=True)
    with jax.named_scope("term_halo"):
        arrived = [from_pair(t, -k) for k, t in ((-2, ta), (-1, tb), (1, td), (2, te))]
    keep, send, spread = split_terms(side, tc, arrived, shares)
    with jax.named_scope("weight_rows"):
        shares = lax.all_to_all(spread, "y", 0, 0, tiled=True)
    with jax.named_scope("term_exchange"):
        swap = [(b ^ 1, b) for b in range(2 * PAIRS)]
        other = lax.ppermute(send, BLK, swap)
    grad_nodes, spread = last_sum(keep, other, shares)
    with jax.named_scope("weight_gather"):
        whole = lax.all_to_all(spread, ring, 0, 0, tiled=True).reshape(RING * SHARE, WIDTH)
    return act, grad_nodes, whole[:HIDDEN].astype(F32), whole[HIDDEN].astype(F32)


def solution(mesh):
    fine = Mesh(
        np.asarray(mesh.devices).reshape(N_Y, N_Z, N_XL, 2, 2), ("y", "z", "xl", "xh", "core")
    )
    placed = (
        P(BLK, COL),
        P(),
        P(COL),
        P(BLK, COL),
        P(BLK, None, None, None, None),
        P(BLK, None, None),
        P(BLK, None, None),
        P(BLK, None),
    )
    return jax.shard_map(
        on_device,
        mesh=fine,
        in_specs=placed,
        out_specs=(P(BLK, COL), P(BLK, COL), P(None, COL), P(COL)),
        check_vma=False,
    )
```

```python
import jax
import jax.numpy as jnp
import numpy as np
from jax import lax
from jax.experimental import pallas as pl
from jax.experimental.pallas import tpu as pltpu
from jax.sharding import Mesh
from jax.sharding import PartitionSpec as P

NODES = 98304
TILE = 128
BLOCKS = 4
ROWS = TILE * BLOCKS
WIDTH = 128
COLS = 4
HIDDEN = WIDTH * COLS
OFFSETS = 9
SLOTS = 16
REACH = 4
N_Y, N_Z, N_XL = 8, 12, 2
PAIRS = N_Y * N_Z
PACK_ROWS = ROWS + 16
RING = N_Z * N_XL
SHARE = 24
BLK = ("y", "z", "xl")
COL = ("xh", "core")
BF16 = jnp.bfloat16
F32 = jnp.float32
VMEM = pl.BlockSpec(memory_space=pltpu.VMEM)
SMEM = pl.BlockSpec(memory_space=pltpu.SMEM)


def params(mib=16):
    return pltpu.CompilerParams(vmem_limit_bytes=mib * 1024 * 1024)


def dense_kernel(codes, slab, dense):
    offset = pl.program_id(0)
    for slot in range(SLOTS):
        code = codes[offset, slot]
        row = pl.multiple_of(((code // BLOCKS) % BLOCKS) * TILE, TILE)
        col = pl.multiple_of((code % BLOCKS) * TILE, TILE)
        tile = slab[0, 0, slot]
        dense[0, pl.ds(row, TILE), pl.ds(col, TILE)] = jnp.where(
            code < BLOCKS * BLOCKS, tile, jnp.zeros_like(tile)
        )


def make_dense(codes, slab):
    return pl.pallas_call(
        dense_kernel,
        grid_spec=pltpu.PrefetchScalarGridSpec(
            num_scalar_prefetch=1,
            grid=(OFFSETS,),
            in_specs=[pl.BlockSpec((1, 1, SLOTS, TILE, TILE), lambda o, _: (0, o, 0, 0, 0))],
            out_specs=pl.BlockSpec((1, ROWS, ROWS), lambda o, _: (o, 0, 0)),
        ),
        out_shape=jax.ShapeDtypeStruct((OFFSETS, ROWS, ROWS), BF16),
        compiler_params=params(),
        cost_estimate=pl.CostEstimate(flops=0, bytes_accessed=10 << 20, transcendentals=0),
        name="dense_tiles",
    )(codes, slab)


def stack_kernel(before, x, after, cots, out):
    del cots
    for i, block in enumerate((before, x, after)):
        out[i] = block[...]


def stack_blocks(before, x, after, cots):
    return pl.pallas_call(
        stack_kernel,
        in_specs=[VMEM] * 3 + [pl.BlockSpec(memory_space=pl.ANY)],
        out_specs=VMEM,
        out_shape=jax.ShapeDtypeStruct((3, ROWS, WIDTH), BF16),
        compiler_params=params(),
        cost_estimate=pl.CostEstimate(flops=0, bytes_accessed=1 << 20, transcendentals=0),
        name="near_blocks",
    )(before, x, after, cots)


def gather_kernel(side, dense, xa, xb, xc, xd, xe, near, far, bias, out):
    total = jnp.zeros((ROWS, WIDTH), F32)
    for k, block in enumerate((xa, xb, xc, xd, xe)):
        total += jnp.dot(dense[2 * k], block[...], preferred_element_type=F32)
    for i in range(3):
        total += jnp.dot(dense[3 + 2 * i - 2 * side[0]], near[i], preferred_element_type=F32)
    total += jnp.dot(dense[1 + 6 * side[0]], far[...], preferred_element_type=F32)
    out[0:ROWS, :] = total.astype(BF16)
    out[ROWS:, :] = jnp.broadcast_to(bias[...], (16, WIDTH))


def gather_rows(side, dense, plane, near, far, bias):
    return pl.pallas_call(
        gather_kernel,
        in_specs=[SMEM] + [VMEM] * 9,
        out_specs=VMEM,
        out_shape=jax.ShapeDtypeStruct((PACK_ROWS, WIDTH), BF16),
        compiler_params=params(),
        cost_estimate=pl.CostEstimate(
            flops=2 * OFFSETS * ROWS * ROWS * WIDTH, bytes_accessed=8 << 20, transcendentals=0
        ),
        name="aggregate_features",
    )(side, dense, *plane, near, far, bias)


def middle_kernel(
    place, mixed, cots, weight, dense,
    act, part, near, far, ta, tb, tc, td, te,
    act_all, grad_all, feats,
):
    side = place[0]
    mine = pl.multiple_of(place[1] * WIDTH, WIDTH)
    bias = jnp.concatenate([mixed[c, ROWS:, :] for c in range(COLS)], axis=1)[0:1].astype(F32)
    step = 128
    for i in range(ROWS // step):
        span = slice(i * step, (i + 1) * step)
        own = jnp.concatenate([mixed[c, span, :] for c in range(COLS)], axis=1)
        feats[span, :] = own
        preact = jnp.dot(own, weight[...], preferred_element_type=F32) + bias
        sig = 1.0 / (1.0 + jnp.exp(-preact))
        act_all[span, :] = (preact * sig).astype(BF16)
        cot = jnp.concatenate([cots[c, span, :] for c in range(COLS)], axis=1)
        grad_all[span, :] = (
            cot.astype(F32) * sig * (1.0 + preact * (1.0 - sig))
        ).astype(BF16)
    act[...] = act_all[:, pl.ds(mine, WIDTH)]
    grad_mine = grad_all[:, pl.ds(mine, WIDTH)].astype(F32)
    weight_grad = jnp.dot(
        grad_mine.T.astype(BF16), feats[...], preferred_element_type=F32
    )
    part[0:ROWS, :] = weight_grad.T
    first = lax.broadcasted_iota(jnp.int32, (RING * SHARE - HIDDEN, WIDTH), 0) == 0
    part[ROWS:, :] = jnp.where(first, jnp.sum(grad_mine, axis=0, keepdims=True), 0.0)
    back = lax.dot_general(
        weight[pl.ds(mine, WIDTH), :],
        grad_all[...],
        (((1,), (1,)), ((), ())),
        preferred_element_type=F32,
    ).astype(BF16)
    for k, term in enumerate((ta, tb, tc, td, te)):
        term[...] = jnp.dot(back, dense[2 * k], preferred_element_type=F32).astype(BF16)
    for i in range(3):
        near[i] = jnp.dot(
            back, dense[3 + 2 * i - 2 * side], preferred_element_type=F32
        ).astype(BF16)
    far[...] = jnp.dot(back, dense[1 + 6 * side], preferred_element_type=F32).astype(BF16)


def middle(place, mixed, cots, weight, dense):
    term = jax.ShapeDtypeStruct((WIDTH, ROWS), BF16)
    return pl.pallas_call(
        middle_kernel,
        in_specs=[SMEM] + [VMEM] * 4,
        out_specs=[VMEM] * 9,
        out_shape=[
            jax.ShapeDtypeStruct((ROWS, WIDTH), BF16),
            jax.ShapeDtypeStruct((RING * SHARE, WIDTH), F32),
            jax.ShapeDtypeStruct((3, WIDTH, ROWS), BF16),
        ]
        + [term] * 6,
        scratch_shapes=[pltpu.VMEM((ROWS, HIDDEN), BF16)] * 3,
        compiler_params=params(),
        cost_estimate=pl.CostEstimate(
            flops=2 * (OFFSETS + 9) * ROWS * ROWS * WIDTH, bytes_accessed=10 << 20, transcendentals=ROWS * HIDDEN
        ),
        name="activation_and_terms",
    )(place, mixed, cots, weight, dense)


def near_kernel(tb, tc, td, near, ra, re, rf, shares, before, keep, after, spread):
    before[...] = (tb[...].astype(F32) + near[0].astype(F32)).astype(BF16)
    total = tc[...].astype(F32) + near[1].astype(F32)
    for arrived in (ra, re, rf):
        total += arrived[...].astype(F32)
    keep[...] = total
    after[...] = (td[...].astype(F32) + near[2].astype(F32)).astype(BF16)
    spread[...] = jnp.broadcast_to(jnp.sum(shares[...], axis=0)[None], spread.shape)


def near_sums(tb, tc, td, near, arrived, shares):
    term = jax.ShapeDtypeStruct((WIDTH, ROWS), BF16)
    return pl.pallas_call(
        near_kernel,
        in_specs=[VMEM] * 8,
        out_specs=[VMEM] * 4,
        out_shape=[
            term,
            jax.ShapeDtypeStruct((WIDTH, ROWS), F32),
            term,
            jax.ShapeDtypeStruct((N_Y, SHARE, WIDTH), F32),
        ],
        compiler_params=params(),
        cost_estimate=pl.CostEstimate(flops=1 << 20, bytes_accessed=2 << 20, transcendentals=0),
        name="near_sums",
    )(tb, tc, td, near, *arrived, shares)


def last_kernel(keep, rb, rd, shares, out, spread):
    total = keep[...] + rb[...].astype(F32) + rd[...].astype(F32)
    out[...] = total.T.astype(BF16)
    share = jnp.sum(shares[...], axis=0) * (1.0 / jnp.sqrt(F32(NODES)))
    spread[...] = jnp.broadcast_to(share.astype(BF16)[None], spread.shape)


def last_sum(keep, arrived, shares):
    return pl.pallas_call(
        last_kernel,
        in_specs=[VMEM] * 4,
        out_specs=[VMEM] * 2,
        out_shape=[
            jax.ShapeDtypeStruct((ROWS, WIDTH), BF16),
            jax.ShapeDtypeStruct((RING, SHARE, WIDTH), BF16),
        ],
        compiler_params=params(),
        cost_estimate=pl.CostEstimate(flops=1 << 17, bytes_accessed=1 << 19, transcendentals=0),
        name="node_gradient",
    )(keep, *arrived, shares)


def widen_kernel(whole, weight_grad, bias_grad):
    weight_grad[...] = whole[0:HIDDEN, :].astype(F32)
    bias_grad[...] = whole[HIDDEN : HIDDEN + 16, :].astype(F32)[0:1]


def widen(whole):
    return pl.pallas_call(
        widen_kernel,
        in_specs=[VMEM],
        out_specs=[VMEM] * 2,
        out_shape=[
            jax.ShapeDtypeStruct((HIDDEN, WIDTH), F32),
            jax.ShapeDtypeStruct((1, WIDTH), F32),
        ],
        compiler_params=params(),
        name="weight_gradient",
    )(whole)


def from_pair(block, hops):
    route = [
        (2 * ((p + hops) % PAIRS) + s, 2 * p + s) for p in range(PAIRS) for s in range(2)
    ]
    return lax.ppermute(block, BLK, route)


def routed(block, source):
    route = []
    for p in range(PAIRS):
        for s in range(2):
            pair, other = source(p, s)
            route.append((2 * (pair % PAIRS) + other, 2 * p + s))
    return lax.ppermute(block, BLK, route)


def on_device(node_feats, weight, layer_bias, cotangent, adj_tiles, tile_row, tile_col, tile_count):
    side = lax.axis_index("xl").astype(jnp.int32)
    column = lax.axis_index(COL).astype(jnp.int32)
    slots = jnp.arange(SLOTS, dtype=jnp.int32)[None, :]
    dead = slots >= tile_count[0][:, None]
    codes = tile_row[0] * BLOCKS + tile_col[0] + BLOCKS * BLOCKS * dead.astype(jnp.int32)

    with jax.named_scope("column_gather"):
        cots = lax.all_gather(cotangent, COL, axis=0, tiled=False)
    with jax.named_scope("feature_halo"):
        x = node_feats
        before, after = from_pair(x, -1), from_pair(x, 1)
        far_before, far_after = from_pair(x, -2), from_pair(x, 2)
        far = routed(x, lambda p, s: (p - 2 + 4 * s, 1 - s))
        near = stack_blocks(before, x, after, cots)
        near = routed(near, lambda p, s: (p, 1 - s))
    dense = make_dense(codes, adj_tiles)
    plane = (far_before, before, x, after, far_after)
    mine = gather_rows(side.reshape(1), dense, plane, near, far, layer_bias.reshape(1, WIDTH))
    with jax.named_scope("column_gather"):
        mixed = lax.all_gather(mine, COL, axis=0, tiled=False)
    act, part, near, far, ta, tb, tc, td, te = middle(
        jnp.stack([side, column]), mixed, cots, weight, dense
    )

    ring = ("z", "xl")
    with jax.named_scope("weight_scatter"):
        shares = lax.all_to_all(part.reshape(RING, SHARE, WIDTH), ring, 0, 0, tiled=True)
    with jax.named_scope("term_halo"):
        near = routed(near, lambda p, s: (p, 1 - s))
        ra, re = from_pair(ta, 2), from_pair(te, -2)
        rf = routed(far, lambda p, s: (p - 2 + 4 * s, 1 - s))
    before, keep, after, spread = near_sums(tb, tc, td, near, (ra, re, rf), shares)
    with jax.named_scope("weight_rows"):
        shares = lax.all_to_all(spread, "y", 0, 0, tiled=True)
    with jax.named_scope("term_halo"):
        rb, rd = from_pair(before, 1), from_pair(after, -1)
    grad_nodes, spread = last_sum(keep, (rb, rd), shares)
    with jax.named_scope("weight_gather"):
        whole = lax.all_to_all(spread, ring, 0, 0, tiled=True).reshape(RING * SHARE, WIDTH)
    weight_grad, bias_grad = widen(whole)
    return act, grad_nodes, weight_grad, bias_grad.reshape(WIDTH)


def solution(mesh):
    fine = Mesh(
        np.asarray(mesh.devices).reshape(N_Y, N_Z, N_XL, 2, 2), ("y", "z", "xl", "xh", "core")
    )
    placed = (
        P(BLK, COL),
        P(),
        P(COL),
        P(BLK, COL),
        P(BLK, None, None, None, None),
        P(BLK, None, None),
        P(BLK, None, None),
        P(BLK, None),
    )
    return jax.shard_map(
        on_device,
        mesh=fine,
        in_specs=placed,
        out_specs=(P(BLK, COL), P(BLK, COL), P(None, COL), P(COL)),
        check_vma=False,
    )
```

```python
import jax
import jax.numpy as jnp
import numpy as np
from jax import lax
from jax.experimental import pallas as pl
from jax.experimental.pallas import tpu as pltpu
from jax.sharding import Mesh
from jax.sharding import PartitionSpec as P

NODES = 98304
TILE = 128
BLOCKS = 4
ROWS = TILE * BLOCKS
WIDTH = 128
COLS = 4
HIDDEN = WIDTH * COLS
OFFSETS = 9
SLOTS = 16
REACH = 4
WINDOW = OFFSETS + 1
N_Y, N_Z, N_XL = 8, 12, 2
PAIRS = N_Y * N_Z
PACK_ROWS = ROWS + 16
RING = N_Z * N_XL
SHARE = 24
BLK = ("y", "z", "xl")
COL = ("xh", "core")
BF16 = jnp.bfloat16
F32 = jnp.float32
VMEM = pl.BlockSpec(memory_space=pltpu.VMEM)
SMEM = pl.BlockSpec(memory_space=pltpu.SMEM)


def params(mib=16):
    return pltpu.CompilerParams(vmem_limit_bytes=mib * 1024 * 1024)


def dense_kernel(side, codes, slab, cots, dense):
    del cots
    left_over = (1 - side[0]) * OFFSETS
    dense[left_over] = jnp.zeros((ROWS, ROWS), BF16)

    @pl.loop(0, OFFSETS)
    def _(offset):
        for slot in range(SLOTS):
            code = codes[offset, slot]
            row = pl.multiple_of(((code >> 2) & 3) * TILE, TILE)
            col = pl.multiple_of((code & 3) * TILE, TILE)
            tile = slab[0, offset, slot]
            dense[offset + side[0], pl.ds(row, TILE), pl.ds(col, TILE)] = jnp.where(
                code < BLOCKS * BLOCKS, tile, jnp.zeros_like(tile)
            )


def make_dense(side, codes, slab, cots):
    return pl.pallas_call(
        dense_kernel,
        in_specs=[SMEM, SMEM, VMEM, pl.BlockSpec(memory_space=pl.ANY)],
        out_specs=VMEM,
        out_shape=jax.ShapeDtypeStruct((WINDOW, ROWS, ROWS), BF16),
        compiler_params=params(),
        cost_estimate=pl.CostEstimate(flops=0, bytes_accessed=10 << 20, transcendentals=0),
        name="dense_tiles",
    )(side, codes, slab, cots)


def gather_kernel(dense, xa, xb, xc, xd, xe, bias, out):
    total = jnp.zeros((ROWS, WIDTH), F32)
    for k, pair in enumerate((xa, xb, xc, xd, xe)):
        for s in range(2):
            total += jnp.dot(dense[2 * k + s], pair[s], preferred_element_type=F32)
    out[0:ROWS, :] = total.astype(BF16)
    out[ROWS:, :] = jnp.broadcast_to(bias[...], (16, WIDTH))


def gather_rows(dense, pairs, bias):
    return pl.pallas_call(
        gather_kernel,
        in_specs=[VMEM] * 7,
        out_specs=VMEM,
        out_shape=jax.ShapeDtypeStruct((PACK_ROWS, WIDTH), BF16),
        compiler_params=params(),
        cost_estimate=pl.CostEstimate(
            flops=2 * WINDOW * ROWS * ROWS * WIDTH, bytes_accessed=8 << 20, transcendentals=0
        ),
        name="aggregate_features",
    )(dense, *pairs, bias)


def middle_kernel(column, mixed, cots, weight, dense, act, part, ta, tb, tc, td, te, act_all, grad_all, feats):
    mine = pl.multiple_of(column[0] * WIDTH, WIDTH)
    bias = jnp.concatenate([mixed[c, ROWS:, :] for c in range(COLS)], axis=1)[0:1].astype(F32)
    step = 128
    for i in range(ROWS // step):
        span = slice(i * step, (i + 1) * step)
        own = jnp.concatenate([mixed[c, span, :] for c in range(COLS)], axis=1)
        feats[span, :] = own
        preact = jnp.dot(own, weight[...], preferred_element_type=F32) + bias
        sig = 1.0 / (1.0 + jnp.exp(-preact))
        act_all[span, :] = (preact * sig).astype(BF16)
        cot = jnp.concatenate([cots[c, span, :] for c in range(COLS)], axis=1)
        grad_all[span, :] = (
            cot.astype(F32) * sig * (1.0 + preact * (1.0 - sig))
        ).astype(BF16)
    act[...] = act_all[:, pl.ds(mine, WIDTH)]
    grad_mine = grad_all[:, pl.ds(mine, WIDTH)].astype(F32)
    weight_grad = jnp.dot(
        grad_mine.T.astype(BF16), feats[...], preferred_element_type=F32
    )
    part[0:ROWS, :] = weight_grad.T
    first = lax.broadcasted_iota(jnp.int32, (RING * SHARE - HIDDEN, WIDTH), 0) == 0
    part[ROWS:, :] = jnp.where(first, jnp.sum(grad_mine, axis=0, keepdims=True), 0.0)
    back = lax.dot_general(
        weight[pl.ds(mine, WIDTH), :],
        grad_all[...],
        (((1,), (1,)), ((), ())),
        preferred_element_type=F32,
    ).astype(BF16)
    for k, pair in enumerate((ta, tb, tc, td, te)):
        for s in range(2):
            pair[s] = jnp.dot(back, dense[2 * k + s], preferred_element_type=F32).astype(BF16)


def middle(column, mixed, cots, weight, dense):
    term = jax.ShapeDtypeStruct((2, WIDTH, ROWS), BF16)
    return pl.pallas_call(
        middle_kernel,
        in_specs=[SMEM] + [VMEM] * 4,
        out_specs=[VMEM] * 7,
        out_shape=[
            jax.ShapeDtypeStruct((ROWS, WIDTH), BF16),
            jax.ShapeDtypeStruct((RING * SHARE, WIDTH), F32),
        ]
        + [term] * 5,
        scratch_shapes=[pltpu.VMEM((ROWS, HIDDEN), BF16)] * 3,
        compiler_params=params(),
        cost_estimate=pl.CostEstimate(
            flops=2 * (WINDOW + 9) * ROWS * ROWS * WIDTH, bytes_accessed=10 << 20, transcendentals=ROWS * HIDDEN
        ),
        name="activation_and_terms",
    )(column, mixed, cots, weight, dense)


def share_kernel(scale, shares, *rest):
    spread = rest[-1]
    total = jnp.sum(shares[...], axis=0) * scale
    spread[...] = jnp.broadcast_to(total.astype(spread.dtype)[None], spread.shape)


def spread_sum(shares, behind, copies, scale, dtype):
    return pl.pallas_call(
        lambda *refs: share_kernel(scale, *refs),
        in_specs=[VMEM] + [pl.BlockSpec(memory_space=pl.ANY)] * len(behind),
        out_specs=VMEM,
        out_shape=jax.ShapeDtypeStruct((copies, SHARE, WIDTH), dtype),
        compiler_params=params(),
        cost_estimate=pl.CostEstimate(flops=1 << 16, bytes_accessed=1 << 19, transcendentals=0),
        name="spread_sum",
    )(shares, *behind)


def split_kernel(side, own, ta, tb, td, te, first, keep, send):
    del first
    for s in range(2):
        total = own[s].astype(F32)
        for arrived in (ta, tb, td, te):
            total += arrived[s].astype(F32)

        @pl.when(side[0] == s)
        def _():
            keep[...] = total

        @pl.when(side[0] != s)
        def _():
            send[...] = total.astype(BF16)


def split_terms(side, own, arrived, first):
    return pl.pallas_call(
        split_kernel,
        in_specs=[SMEM] + [VMEM] * 5 + [pl.BlockSpec(memory_space=pl.ANY)],
        out_specs=[VMEM] * 2,
        out_shape=[
            jax.ShapeDtypeStruct((WIDTH, ROWS), F32),
            jax.ShapeDtypeStruct((WIDTH, ROWS), BF16),
        ],
        compiler_params=params(),
        cost_estimate=pl.CostEstimate(flops=1 << 20, bytes_accessed=2 << 20, transcendentals=0),
        name="pair_sums",
    )(side, own, *arrived, first)


def last_kernel(keep, arrived, first, out):
    del first
    out[...] = (keep[...] + arrived[...].astype(F32)).T.astype(BF16)


def last_sum(keep, arrived, first):
    return pl.pallas_call(
        last_kernel,
        in_specs=[VMEM] * 2 + [pl.BlockSpec(memory_space=pl.ANY)],
        out_specs=VMEM,
        out_shape=jax.ShapeDtypeStruct((ROWS, WIDTH), BF16),
        compiler_params=params(),
        cost_estimate=pl.CostEstimate(flops=1 << 17, bytes_accessed=1 << 19, transcendentals=0),
        name="node_gradient",
    )(keep, arrived, first)


def widen_kernel(whole, weight_grad, bias_grad):
    weight_grad[...] = whole[0:HIDDEN, :].astype(F32)
    bias_grad[...] = whole[HIDDEN : HIDDEN + 16, :].astype(F32)[0:1]


def widen(whole):
    return pl.pallas_call(
        widen_kernel,
        in_specs=[VMEM],
        out_specs=[VMEM] * 2,
        out_shape=[
            jax.ShapeDtypeStruct((HIDDEN, WIDTH), F32),
            jax.ShapeDtypeStruct((1, WIDTH), F32),
        ],
        compiler_params=params(),
        name="weight_gradient",
    )(whole)


def from_pair(block, hops):
    route = [
        (2 * ((p + hops) % PAIRS) + s, 2 * p + s) for p in range(PAIRS) for s in range(2)
    ]
    return lax.ppermute(block, BLK, route)


def on_device(node_feats, weight, layer_bias, cotangent, adj_tiles, tile_row, tile_col, tile_count):
    side = lax.axis_index("xl").astype(jnp.int32).reshape(1)
    column = lax.axis_index(COL).astype(jnp.int32).reshape(1)
    slots = jnp.arange(SLOTS, dtype=jnp.int32)[None, :]
    dead = slots >= tile_count[0][:, None]
    codes = tile_row[0] * BLOCKS + tile_col[0] + BLOCKS * BLOCKS * dead.astype(jnp.int32)

    with jax.named_scope("feature_halo"):
        pair = lax.all_gather(node_feats, "xl", axis=0, tiled=False)
        pairs = [pair if k == 0 else from_pair(pair, k) for k in (-2, -1, 0, 1, 2)]
    with jax.named_scope("column_gather"):
        cots = lax.all_gather(cotangent, COL, axis=0, tiled=False)
    dense = make_dense(side, codes, adj_tiles, cots)
    mine = gather_rows(dense, pairs, layer_bias.reshape(1, WIDTH))
    with jax.named_scope("column_gather"):
        mixed = lax.all_gather(mine, COL, axis=0, tiled=False)
    act, part, ta, tb, tc, td, te = middle(column, mixed, cots, weight, dense)

    ring = ("z", "xl")
    with jax.named_scope("weight_scatter"):
        shares = lax.all_to_all(part.reshape(RING, SHARE, WIDTH), ring, 0, 0, tiled=True)
    with jax.named_scope("term_halo"):
        arrived = [from_pair(t, -k) for k, t in ((-2, ta), (-1, tb), (1, td), (2, te))]
    spread = spread_sum(shares, arrived[1:3], N_Y, 1.0, F32)
    keep, send = split_terms(side, tc, arrived, spread)
    with jax.named_scope("weight_rows"):
        shares = lax.all_to_all(spread, "y", 0, 0, tiled=True)
    with jax.named_scope("term_exchange"):
        swap = [(b ^ 1, b) for b in range(2 * PAIRS)]
        other = lax.ppermute(send, BLK, swap)
    spread = spread_sum(shares, [keep], RING, float(NODES) ** -0.5, BF16)
    grad_nodes = last_sum(keep, other, spread)
    with jax.named_scope("weight_gather"):
        whole = lax.all_to_all(spread, ring, 0, 0, tiled=True).reshape(RING * SHARE, WIDTH)
    weight_grad, bias_grad = widen(whole)
    return act, grad_nodes, weight_grad, bias_grad.reshape(WIDTH)


def solution(mesh):
    fine = Mesh(
        np.asarray(mesh.devices).reshape(N_Y, N_Z, N_XL, 2, 2), ("y", "z", "xl", "xh", "core")
    )
    placed = (
        P(BLK, COL),
        P(),
        P(COL),
        P(BLK, COL),
        P(BLK, None, None, None, None),
        P(BLK, None, None),
        P(BLK, None, None),
        P(BLK, None),
    )
    return jax.shard_map(
        on_device,
        mesh=fine,
        in_specs=placed,
        out_specs=(P(BLK, COL), P(BLK, COL), P(None, COL), P(COL)),
        check_vma=False,
    )
```

```python
import jax
import jax.numpy as jnp
import numpy as np
from jax import lax
from jax.experimental import pallas as pl
from jax.experimental.pallas import tpu as pltpu
from jax.sharding import Mesh
from jax.sharding import PartitionSpec as P

NODES = 98304
TILE = 128
BLOCKS = 4
ROWS = TILE * BLOCKS
WIDTH = 128
COLS = 4
HIDDEN = WIDTH * COLS
OFFSETS = 9
SLOTS = 16
REACH = 4
N_Y, N_Z, N_XL = 8, 12, 2
PAIRS = N_Y * N_Z
PACK_ROWS = ROWS + 16
RING = N_Z * N_XL
SHARE = 24
BLK = ("y", "z", "xl")
COL = ("xh", "core")
BF16 = jnp.bfloat16
F32 = jnp.float32
VMEM = pl.BlockSpec(memory_space=pltpu.VMEM)
SMEM = pl.BlockSpec(memory_space=pltpu.SMEM)


def params(mib=16):
    return pltpu.CompilerParams(vmem_limit_bytes=mib * 1024 * 1024)


def dense_kernel(codes, slab, dense, held, sems):
    copies = [
        pltpu.make_async_copy(slab.at[0, o], held.at[o], sems.at[o]) for o in range(OFFSETS)
    ]
    for copy in copies:
        copy.start()
    for offset, copy in enumerate(copies):
        copy.wait()
        for slot in range(SLOTS):
            code = codes[offset, slot]
            row = pl.multiple_of(((code >> 2) & 3) * TILE, TILE)
            col = pl.multiple_of((code & 3) * TILE, TILE)
            tile = held[offset, slot]
            dense[offset, pl.ds(row, TILE), pl.ds(col, TILE)] = jnp.where(
                code < BLOCKS * BLOCKS, tile, jnp.zeros_like(tile)
            )


def make_dense(codes, slab):
    return pl.pallas_call(
        dense_kernel,
        in_specs=[SMEM, pl.BlockSpec(memory_space=pltpu.HBM)],
        out_specs=VMEM,
        out_shape=jax.ShapeDtypeStruct((OFFSETS, ROWS, ROWS), BF16),
        scratch_shapes=[
            pltpu.VMEM((OFFSETS, SLOTS, TILE, TILE), BF16),
            pltpu.SemaphoreType.DMA((OFFSETS,)),
        ],
        compiler_params=params(),
        cost_estimate=pl.CostEstimate(flops=0, bytes_accessed=10 << 20, transcendentals=0),
        name="dense_tiles",
    )(codes, pltpu.with_memory_space_constraint(slab, pltpu.HBM))


def gather_kernel(side, dense, before, own, after, far, lone, bias, out):
    s = side[0]
    total = jnp.dot(dense[8 - 8 * s], lone[...], preferred_element_type=F32)
    for first, pair in ((2 - s, before), (4 - s, own), (6 - s, after), (7 * s, far)):
        for i in range(2):
            total += jnp.dot(dense[first + i], pair[i], preferred_element_type=F32)
    out[0:ROWS, :] = total.astype(BF16)
    out[ROWS:, :] = jnp.broadcast_to(bias[...], (16, WIDTH))


def gather_rows(side, dense, blocks, bias):
    return pl.pallas_call(
        gather_kernel,
        in_specs=[SMEM] + [VMEM] * 7,
        out_specs=VMEM,
        out_shape=jax.ShapeDtypeStruct((PACK_ROWS, WIDTH), BF16),
        compiler_params=params(),
        cost_estimate=pl.CostEstimate(
            flops=2 * OFFSETS * ROWS * ROWS * WIDTH, bytes_accessed=8 << 20, transcendentals=0
        ),
        name="aggregate_features",
    )(side, dense, *blocks, bias)


def middle_kernel(
    place, mixed, cots, weight, dense,
    act, part, before, own, after, far, lone,
    act_all, grad_all, feats,
):
    side = place[0]
    mine = pl.multiple_of(place[1] * WIDTH, WIDTH)
    bias = jnp.concatenate([mixed[c, ROWS:, :] for c in range(COLS)], axis=1)[0:1].astype(F32)
    step = 128
    for i in range(ROWS // step):
        span = slice(i * step, (i + 1) * step)
        rows = jnp.concatenate([mixed[c, span, :] for c in range(COLS)], axis=1)
        feats[span, :] = rows
        preact = jnp.dot(rows, weight[...], preferred_element_type=F32) + bias
        sig = 1.0 / (1.0 + jnp.exp(-preact))
        act_all[span, :] = (preact * sig).astype(BF16)
        cot = jnp.concatenate([cots[c, span, :] for c in range(COLS)], axis=1)
        grad_all[span, :] = (
            cot.astype(F32) * sig * (1.0 + preact * (1.0 - sig))
        ).astype(BF16)
    act[...] = act_all[:, pl.ds(mine, WIDTH)]
    grad_mine = grad_all[:, pl.ds(mine, WIDTH)].astype(F32)
    weight_grad = jnp.dot(
        grad_mine.T.astype(BF16), feats[...], preferred_element_type=F32
    )
    part[0:ROWS, :] = weight_grad.T
    first = lax.broadcasted_iota(jnp.int32, (RING * SHARE - HIDDEN, WIDTH), 0) == 0
    part[ROWS:, :] = jnp.where(first, jnp.sum(grad_mine, axis=0, keepdims=True), 0.0)
    back = lax.dot_general(
        weight[pl.ds(mine, WIDTH), :],
        grad_all[...],
        (((1,), (1,)), ((), ())),
        preferred_element_type=F32,
    ).astype(BF16)
    for first, pair in (
        (2 - side, before), (4 - side, own), (6 - side, after), (7 * side, far)
    ):
        for i in range(2):
            pair[i] = jnp.dot(back, dense[first + i], preferred_element_type=F32).astype(BF16)
    lone[...] = jnp.dot(back, dense[8 - 8 * side], preferred_element_type=F32).astype(BF16)


def middle(place, mixed, cots, weight, dense):
    pair = jax.ShapeDtypeStruct((2, WIDTH, ROWS), BF16)
    return pl.pallas_call(
        middle_kernel,
        in_specs=[SMEM] + [VMEM] * 4,
        out_specs=[VMEM] * 7,
        out_shape=[
            jax.ShapeDtypeStruct((ROWS, WIDTH), BF16),
            jax.ShapeDtypeStruct((RING * SHARE, WIDTH), F32),
        ]
        + [pair] * 4
        + [jax.ShapeDtypeStruct((WIDTH, ROWS), BF16)],
        scratch_shapes=[pltpu.VMEM((ROWS, HIDDEN), BF16)] * 3,
        compiler_params=params(),
        cost_estimate=pl.CostEstimate(
            flops=2 * (OFFSETS + 9) * ROWS * ROWS * WIDTH, bytes_accessed=10 << 20, transcendentals=ROWS * HIDDEN
        ),
        name="activation_and_terms",
    )(place, mixed, cots, weight, dense)


def share_kernel(scale, shares, *rest):
    spread = rest[-1]
    total = jnp.sum(shares[...], axis=0) * scale
    spread[...] = jnp.broadcast_to(total.astype(spread.dtype)[None], spread.shape)


def spread_sum(shares, behind, copies, scale, dtype):
    return pl.pallas_call(
        lambda *refs: share_kernel(scale, *refs),
        in_specs=[VMEM] + [pl.BlockSpec(memory_space=pl.ANY)] * len(behind),
        out_specs=VMEM,
        out_shape=jax.ShapeDtypeStruct((copies, SHARE, WIDTH), dtype),
        compiler_params=params(),
        cost_estimate=pl.CostEstimate(flops=1 << 16, bytes_accessed=1 << 19, transcendentals=0),
        name="spread_sum",
    )(shares, *behind)


def split_kernel(side, own, before, after, far, lone, first, keep, send):
    del first
    for s in range(2):
        total = own[s].astype(F32)
        for arrived in (before, after, far):
            total += arrived[s].astype(F32)

        @pl.when(side[0] == s)
        def _():
            keep[...] = total + lone[...].astype(F32)

        @pl.when(side[0] != s)
        def _():
            send[...] = total.astype(BF16)


def split_terms(side, own, arrived, first):
    return pl.pallas_call(
        split_kernel,
        in_specs=[SMEM] + [VMEM] * 5 + [pl.BlockSpec(memory_space=pl.ANY)],
        out_specs=[VMEM] * 2,
        out_shape=[
            jax.ShapeDtypeStruct((WIDTH, ROWS), F32),
            jax.ShapeDtypeStruct((WIDTH, ROWS), BF16),
        ],
        compiler_params=params(),
        cost_estimate=pl.CostEstimate(flops=1 << 20, bytes_accessed=2 << 20, transcendentals=0),
        name="pair_sums",
    )(side, own, *arrived, first)


def last_kernel(keep, arrived, first, out):
    del first
    out[...] = (keep[...] + arrived[...].astype(F32)).T.astype(BF16)


def last_sum(keep, arrived, first):
    return pl.pallas_call(
        last_kernel,
        in_specs=[VMEM] * 2 + [pl.BlockSpec(memory_space=pl.ANY)],
        out_specs=VMEM,
        out_shape=jax.ShapeDtypeStruct((ROWS, WIDTH), BF16),
        compiler_params=params(),
        cost_estimate=pl.CostEstimate(flops=1 << 17, bytes_accessed=1 << 19, transcendentals=0),
        name="node_gradient",
    )(keep, arrived, first)


def widen_kernel(whole, weight_grad, bias_grad):
    weight_grad[...] = whole[0:HIDDEN, :].astype(F32)
    bias_grad[...] = whole[HIDDEN : HIDDEN + 16, :].astype(F32)[0:1]


def widen(whole):
    return pl.pallas_call(
        widen_kernel,
        in_specs=[VMEM],
        out_specs=[VMEM] * 2,
        out_shape=[
            jax.ShapeDtypeStruct((HIDDEN, WIDTH), F32),
            jax.ShapeDtypeStruct((1, WIDTH), F32),
        ],
        compiler_params=params(),
        name="weight_gradient",
    )(whole)


def routed(block, source):
    route = []
    for p in range(PAIRS):
        for s in range(2):
            pair, other = source(p, s)
            route.append((2 * (pair % PAIRS) + other, 2 * p + s))
    return lax.ppermute(block, BLK, route)


def on_device(node_feats, weight, layer_bias, cotangent, adj_tiles, tile_row, tile_col, tile_count):
    side = lax.axis_index("xl").astype(jnp.int32).reshape(1)
    column = lax.axis_index(COL).astype(jnp.int32).reshape(1)
    slots = jnp.arange(SLOTS, dtype=jnp.int32)[None, :]
    dead = slots >= tile_count[0][:, None]
    codes = tile_row[0] * BLOCKS + tile_col[0] + BLOCKS * BLOCKS * dead.astype(jnp.int32)

    with jax.named_scope("feature_halo"):
        lone = routed(node_feats, lambda p, s: (p + 2 - 4 * s, s))
        pair = lax.all_gather(node_feats, "xl", axis=0, tiled=False)
        far = routed(pair, lambda p, s: (p - 2 + 4 * s, s))
        before = routed(pair, lambda p, s: (p - 1, s))
        after = routed(pair, lambda p, s: (p + 1, s))
    with jax.named_scope("column_gather"):
        cots = lax.all_gather(cotangent, COL, axis=0, tiled=False)
    dense = make_dense(codes, adj_tiles)
    mine = gather_rows(side, dense, (before, pair, after, far, lone), layer_bias.reshape(1, WIDTH))
    with jax.named_scope("column_gather"):
        mixed = lax.all_gather(mine, COL, axis=0, tiled=False)
    act, part, before, own, after, far, lone = middle(
        jnp.concatenate([side, column]), mixed, cots, weight, dense
    )

    ring = ("z", "xl")
    with jax.named_scope("weight_scatter"):
        shares = lax.all_to_all(part.reshape(RING, SHARE, WIDTH), ring, 0, 0, tiled=True)
    with jax.named_scope("term_halo"):
        before = routed(before, lambda p, s: (p + 1, s))
        after = routed(after, lambda p, s: (p - 1, s))
        far = routed(far, lambda p, s: (p + 2 - 4 * s, s))
        lone = routed(lone, lambda p, s: (p - 2 + 4 * s, s))
    spread = spread_sum(shares, [before], N_Y, 1.0, F32)
    keep, send = split_terms(side, own, (before, after, far, lone), spread)
    with jax.named_scope("weight_rows"):
        shares = lax.all_to_all(spread, "y", 0, 0, tiled=True)
    with jax.named_scope("term_exchange"):
        other = routed(send, lambda p, s: (p, 1 - s))
    spread = spread_sum(shares, [keep], RING, float(NODES) ** -0.5, BF16)
    grad_nodes = last_sum(keep, other, spread)
    with jax.named_scope("weight_gather"):
        whole = lax.all_to_all(spread, ring, 0, 0, tiled=True).reshape(RING * SHARE, WIDTH)
    weight_grad, bias_grad = widen(whole)
    return act, grad_nodes, weight_grad, bias_grad.reshape(WIDTH)


def solution(mesh):
    fine = Mesh(
        np.asarray(mesh.devices).reshape(N_Y, N_Z, N_XL, 2, 2), ("y", "z", "xl", "xh", "core")
    )
    placed = (
        P(BLK, COL),
        P(),
        P(COL),
        P(BLK, COL),
        P(BLK, None, None, None, None),
        P(BLK, None, None),
        P(BLK, None, None),
        P(BLK, None),
    )
    return jax.shard_map(
        on_device,
        mesh=fine,
        in_specs=placed,
        out_specs=(P(BLK, COL), P(BLK, COL), P(None, COL), P(COL)),
        check_vma=False,
    )
```

```python
import jax
import jax.numpy as jnp
import numpy as np
from jax import lax
from jax.experimental import pallas as pl
from jax.experimental.pallas import tpu as pltpu
from jax.sharding import Mesh
from jax.sharding import PartitionSpec as P

NODES = 98304
TILE = 128
BLOCKS = 4
ROWS = TILE * BLOCKS
WIDTH = 128
COLS = 4
HIDDEN = WIDTH * COLS
OFFSETS = 9
SLOTS = 16
REACH = 4
N_Y, N_Z, N_XL = 8, 12, 2
GROUP = 4
PAIRS = N_Y * N_Z
PACK_ROWS = ROWS + 16
RING = N_Z * N_XL
SHARE = 24
BLK = ("y", "zq", "zp", "xl")
FOUR = ("zp", "xl")
COL = ("xh", "core")
BF16 = jnp.bfloat16
F32 = jnp.float32
VMEM = pl.BlockSpec(memory_space=pltpu.VMEM)
SMEM = pl.BlockSpec(memory_space=pltpu.SMEM)


def params(mib=16):
    return pltpu.CompilerParams(vmem_limit_bytes=mib * 1024 * 1024)


def dense_kernel(codes, slab, dense, held, sems):
    copies = [
        pltpu.make_async_copy(slab.at[0, o], held.at[o], sems.at[o]) for o in range(OFFSETS)
    ]
    for copy in copies:
        copy.start()
    dense[0] = jnp.zeros((ROWS, ROWS), BF16)
    dense[OFFSETS + 1] = jnp.zeros((ROWS, ROWS), BF16)
    for offset, copy in enumerate(copies):
        copy.wait()
        for slot in range(SLOTS):
            code = codes[offset, slot]
            row = pl.multiple_of(((code >> 2) & 3) * TILE, TILE)
            col = pl.multiple_of((code & 3) * TILE, TILE)
            tile = held[offset, slot]
            dense[offset + 1, pl.ds(row, TILE), pl.ds(col, TILE)] = jnp.where(
                code < BLOCKS * BLOCKS, tile, jnp.zeros_like(tile)
            )


def make_dense(codes, slab):
    return pl.pallas_call(
        dense_kernel,
        in_specs=[SMEM, pl.BlockSpec(memory_space=pltpu.HBM)],
        out_specs=VMEM,
        out_shape=jax.ShapeDtypeStruct((OFFSETS + 2, ROWS, ROWS), BF16),
        scratch_shapes=[
            pltpu.VMEM((OFFSETS, SLOTS, TILE, TILE), BF16),
            pltpu.SemaphoreType.DMA((OFFSETS,)),
        ],
        compiler_params=params(),
        cost_estimate=pl.CostEstimate(flops=0, bytes_accessed=10 << 20, transcendentals=0),
        name="dense_tiles",
    )(codes, pltpu.with_memory_space_constraint(slab, pltpu.HBM))


def starts(member):
    upper = member // 2
    return 5 - member, 1 + 8 * upper - member, 9 - 6 * upper - member


def gather_kernel(member, dense, own, beside, beyond, bias, out):
    total = jnp.zeros((ROWS, WIDTH), F32)
    for first, blocks in zip(starts(member[0]), (own, beside, beyond)):
        for i in range(blocks.shape[0]):
            total += jnp.dot(dense[first + i], blocks[i], preferred_element_type=F32)
    out[0:ROWS, :] = total.astype(BF16)
    out[ROWS:, :] = jnp.broadcast_to(bias[...], (16, WIDTH))


def gather_rows(member, dense, blocks, bias):
    return pl.pallas_call(
        gather_kernel,
        in_specs=[SMEM] + [VMEM] * 5,
        out_specs=VMEM,
        out_shape=jax.ShapeDtypeStruct((PACK_ROWS, WIDTH), BF16),
        compiler_params=params(),
        cost_estimate=pl.CostEstimate(
            flops=2 * OFFSETS * ROWS * ROWS * WIDTH, bytes_accessed=8 << 20, transcendentals=0
        ),
        name="aggregate_features",
    )(member, dense, *blocks, bias)


def middle_kernel(
    place, mixed, cots, weight, dense,
    act, part, own, beside, beyond,
    act_all, grad_all, feats,
):
    mine = pl.multiple_of(place[1] * WIDTH, WIDTH)
    bias = jnp.concatenate([mixed[c, ROWS:, :] for c in range(COLS)], axis=1)[0:1].astype(F32)
    step = 128
    for i in range(ROWS // step):
        span = slice(i * step, (i + 1) * step)
        rows = jnp.concatenate([mixed[c, span, :] for c in range(COLS)], axis=1)
        feats[span, :] = rows
        preact = jnp.dot(rows, weight[...], preferred_element_type=F32) + bias
        sig = 1.0 / (1.0 + jnp.exp(-preact))
        act_all[span, :] = (preact * sig).astype(BF16)
        cot = jnp.concatenate([cots[c, span, :] for c in range(COLS)], axis=1)
        grad_all[span, :] = (
            cot.astype(F32) * sig * (1.0 + preact * (1.0 - sig))
        ).astype(BF16)
    act[...] = act_all[:, pl.ds(mine, WIDTH)]
    grad_mine = grad_all[:, pl.ds(mine, WIDTH)].astype(F32)
    weight_grad = jnp.dot(
        grad_mine.T.astype(BF16), feats[...], preferred_element_type=F32
    )
    part[0:ROWS, :] = weight_grad.T
    first = lax.broadcasted_iota(jnp.int32, (RING * SHARE - HIDDEN, WIDTH), 0) == 0
    part[ROWS:, :] = jnp.where(first, jnp.sum(grad_mine, axis=0, keepdims=True), 0.0)
    back = lax.dot_general(
        weight[pl.ds(mine, WIDTH), :],
        grad_all[...],
        (((1,), (1,)), ((), ())),
        preferred_element_type=F32,
    ).astype(BF16)
    for first, terms in zip(starts(place[0]), (own, beside, beyond)):
        for i in range(terms.shape[0]):
            terms[i] = jnp.dot(back, dense[first + i], preferred_element_type=F32).astype(BF16)


def middle(place, mixed, cots, weight, dense):
    return pl.pallas_call(
        middle_kernel,
        in_specs=[SMEM] + [VMEM] * 4,
        out_specs=[VMEM] * 5,
        out_shape=[
            jax.ShapeDtypeStruct((ROWS, WIDTH), BF16),
            jax.ShapeDtypeStruct((RING * SHARE, WIDTH), F32),
        ]
        + [jax.ShapeDtypeStruct((n, WIDTH, ROWS), BF16) for n in (GROUP, GROUP, 2)],
        scratch_shapes=[pltpu.VMEM((ROWS, HIDDEN), BF16)] * 3,
        compiler_params=params(),
        cost_estimate=pl.CostEstimate(
            flops=2 * (OFFSETS + 9) * ROWS * ROWS * WIDTH, bytes_accessed=10 << 20, transcendentals=ROWS * HIDDEN
        ),
        name="activation_and_terms",
    )(place, mixed, cots, weight, dense)


def share_kernel(scale, shares, *rest):
    spread = rest[-1]
    total = jnp.sum(shares[...], axis=0) * scale
    spread[...] = jnp.broadcast_to(total.astype(spread.dtype)[None], spread.shape)


def spread_sum(shares, behind, copies, scale, dtype):
    return pl.pallas_call(
        lambda *refs: share_kernel(scale, *refs),
        in_specs=[VMEM] + [pl.BlockSpec(memory_space=pl.ANY)] * len(behind),
        out_specs=VMEM,
        out_shape=jax.ShapeDtypeStruct((copies, SHARE, WIDTH), dtype),
        compiler_params=params(),
        cost_estimate=pl.CostEstimate(flops=1 << 16, bytes_accessed=1 << 19, transcendentals=0),
        name="spread_sum",
    )(shares, *behind)


def split_kernel(member, own, beside, beyond, first, keep, send):
    del first
    side, upper = member[0] % 2, member[0] // 2
    for i in range(GROUP):
        total = own[i].astype(F32) + beside[i].astype(F32)
        total += jnp.where(upper == i // 2, beyond[i % 2].astype(F32), 0.0)

        @pl.when(side == i % 2)
        def _():
            keep[i // 2] = total

        @pl.when(side != i % 2)
        def _():
            send[i // 2] = total.astype(BF16)


def split_terms(member, own, arrived, first):
    return pl.pallas_call(
        split_kernel,
        in_specs=[SMEM] + [VMEM] * 3 + [pl.BlockSpec(memory_space=pl.ANY)],
        out_specs=[VMEM] * 2,
        out_shape=[
            jax.ShapeDtypeStruct((2, WIDTH, ROWS), F32),
            jax.ShapeDtypeStruct((2, WIDTH, ROWS), BF16),
        ],
        compiler_params=params(),
        cost_estimate=pl.CostEstimate(flops=1 << 20, bytes_accessed=2 << 20, transcendentals=0),
        name="group_sums",
    )(member, own, *arrived, first)


def halve_kernel(member, mine, arrived, keep, send):
    upper = member[0] // 2
    keep[...] = mine[upper] + arrived[upper].astype(F32)
    send[...] = (mine[1 - upper] + arrived[1 - upper].astype(F32)).astype(BF16)


def halve_terms(member, mine, arrived):
    return pl.pallas_call(
        halve_kernel,
        in_specs=[SMEM] + [VMEM] * 2,
        out_specs=[VMEM] * 2,
        out_shape=[
            jax.ShapeDtypeStruct((WIDTH, ROWS), F32),
            jax.ShapeDtypeStruct((WIDTH, ROWS), BF16),
        ],
        compiler_params=params(),
        cost_estimate=pl.CostEstimate(flops=1 << 18, bytes_accessed=1 << 20, transcendentals=0),
        name="side_sums",
    )(member, mine, arrived)


def last_kernel(keep, arrived, first, out):
    del first
    out[...] = (keep[...] + arrived[...].astype(F32)).T.astype(BF16)


def last_sum(keep, arrived, first):
    return pl.pallas_call(
        last_kernel,
        in_specs=[VMEM] * 2 + [pl.BlockSpec(memory_space=pl.ANY)],
        out_specs=VMEM,
        out_shape=jax.ShapeDtypeStruct((ROWS, WIDTH), BF16),
        compiler_params=params(),
        cost_estimate=pl.CostEstimate(flops=1 << 17, bytes_accessed=1 << 19, transcendentals=0),
        name="node_gradient",
    )(keep, arrived, first)


def widen_kernel(whole, weight_grad, bias_grad):
    weight_grad[...] = whole[0:HIDDEN, :].astype(F32)
    bias_grad[...] = whole[HIDDEN : HIDDEN + 16, :].astype(F32)[0:1]


def widen(whole):
    return pl.pallas_call(
        widen_kernel,
        in_specs=[VMEM],
        out_specs=[VMEM] * 2,
        out_shape=[
            jax.ShapeDtypeStruct((HIDDEN, WIDTH), F32),
            jax.ShapeDtypeStruct((1, WIDTH), F32),
        ],
        compiler_params=params(),
        name="weight_gradient",
    )(whole)


def routed(block, source):
    route = []
    for p in range(PAIRS):
        for s in range(2):
            pair, other = source(p, s)
            route.append((2 * (pair % PAIRS) + other, 2 * p + s))
    return lax.ppermute(block, BLK, route)


def on_device(node_feats, weight, layer_bias, cotangent, adj_tiles, tile_row, tile_col, tile_count):
    member = lax.axis_index(FOUR).astype(jnp.int32).reshape(1)
    column = lax.axis_index(COL).astype(jnp.int32).reshape(1)
    slots = jnp.arange(SLOTS, dtype=jnp.int32)[None, :]
    dead = slots >= tile_count[0][:, None]
    codes = tile_row[0] * BLOCKS + tile_col[0] + BLOCKS * BLOCKS * dead.astype(jnp.int32)

    def one_away(block):
        return routed(block, lambda p, s: (p - 1 + 2 * (p % 2), s))

    with jax.named_scope("feature_halo"):
        four = lax.all_gather(node_feats, FOUR, axis=0, tiled=False)
        beside = one_away(four)
        pair = lax.dynamic_slice_in_dim(four, 2 * lax.axis_index("zp"), 2, 0)
        beyond = routed(pair, lambda p, s: (p + 2 - 4 * (p % 2), s))
    with jax.named_scope("column_gather"):
        cots = lax.all_gather(cotangent, COL, axis=0, tiled=False)
    dense = make_dense(codes, adj_tiles)
    mine = gather_rows(member, dense, (four, beside, beyond), layer_bias.reshape(1, WIDTH))
    with jax.named_scope("column_gather"):
        mixed = lax.all_gather(mine, COL, axis=0, tiled=False)
    act, part, own, beside, beyond = middle(
        jnp.concatenate([member, column]), mixed, cots, weight, dense
    )

    ring = ("zq", "zp", "xl")
    with jax.named_scope("weight_scatter"):
        shares = lax.all_to_all(part.reshape(RING, SHARE, WIDTH), ring, 0, 0, tiled=True)
    with jax.named_scope("term_halo"):
        beside = one_away(beside)
        beyond = routed(beyond, lambda p, s: (p - 2 + 4 * (p % 2), s))
    spread = spread_sum(shares, [beside], N_Y, 1.0, F32)
    keep, send = split_terms(member, own, (beside, beyond), spread)
    with jax.named_scope("weight_rows"):
        shares = lax.all_to_all(spread, "y", 0, 0, tiled=True)
    spread = spread_sum(shares, [keep], RING, float(NODES) ** -0.5, BF16)
    with jax.named_scope("term_exchange"):
        keep, send = halve_terms(member, keep, routed(send, lambda p, s: (p, 1 - s)))
        other = routed(send, lambda p, s: (p + 1 - 2 * (p % 2), s))
    grad_nodes = last_sum(keep, other, spread)
    with jax.named_scope("weight_gather"):
        whole = lax.all_to_all(spread, ring, 0, 0, tiled=True).reshape(RING * SHARE, WIDTH)
    weight_grad, bias_grad = widen(whole)
    return act, grad_nodes, weight_grad, bias_grad.reshape(WIDTH)


def solution(mesh):
    fine = Mesh(
        np.asarray(mesh.devices).reshape(N_Y, N_Z // 2, 2, N_XL, 2, 2), BLK + COL
    )
    placed = (
        P(BLK, COL),
        P(),
        P(COL),
        P(BLK, COL),
        P(BLK, None, None, None, None),
        P(BLK, None, None),
        P(BLK, None, None),
        P(BLK, None),
    )
    return jax.shard_map(
        on_device,
        mesh=fine,
        in_specs=placed,
        out_specs=(P(BLK, COL), P(BLK, COL), P(None, COL), P(COL)),
        check_vma=False,
    )
```

```python
import jax
import jax.numpy as jnp
import numpy as np
from jax import lax
from jax.experimental import pallas as pl
from jax.experimental.pallas import tpu as pltpu
from jax.sharding import Mesh
from jax.sharding import PartitionSpec as P

NODES = 98304
TILE = 128
BLOCKS = 4
ROWS = TILE * BLOCKS
WIDTH = 128
COLS = 4
HIDDEN = WIDTH * COLS
OFFSETS = 9
SLOTS = 16
REACH = 4
N_Y, N_Z, N_XL = 8, 12, 2
PAIRS = N_Y * N_Z
PACK_ROWS = ROWS + 16
RING = N_Z * N_XL
SHARE = 24
BLK = ("y", "zq", "zp", "xl")
FOUR = ("zp", "xl")
COL = ("xh", "core")
BF16 = jnp.bfloat16
F32 = jnp.float32
VMEM = pl.BlockSpec(memory_space=pltpu.VMEM)
SMEM = pl.BlockSpec(memory_space=pltpu.SMEM)


def params(mib=16):
    return pltpu.CompilerParams(vmem_limit_bytes=mib * 1024 * 1024)


def dense_kernel(codes, slab, dense, held, sems):
    copies = [
        pltpu.make_async_copy(slab.at[0, o], held.at[o], sems.at[o]) for o in range(OFFSETS)
    ]
    for copy in copies:
        copy.start()
    dense[0] = jnp.zeros((ROWS, ROWS), BF16)
    dense[OFFSETS + 1] = jnp.zeros((ROWS, ROWS), BF16)
    for offset, copy in enumerate(copies):
        copy.wait()
        for slot in range(SLOTS):
            code = codes[offset, slot]
            row = pl.multiple_of(((code >> 2) & 3) * TILE, TILE)
            col = pl.multiple_of((code & 3) * TILE, TILE)
            tile = held[offset, slot]
            dense[offset + 1, pl.ds(row, TILE), pl.ds(col, TILE)] = jnp.where(
                code < BLOCKS * BLOCKS, tile, jnp.zeros_like(tile)
            )


def make_dense(codes, slab):
    return pl.pallas_call(
        dense_kernel,
        in_specs=[SMEM, pl.BlockSpec(memory_space=pltpu.HBM)],
        out_specs=VMEM,
        out_shape=jax.ShapeDtypeStruct((OFFSETS + 2, ROWS, ROWS), BF16),
        scratch_shapes=[
            pltpu.VMEM((OFFSETS, SLOTS, TILE, TILE), BF16),
            pltpu.SemaphoreType.DMA((OFFSETS,)),
        ],
        compiler_params=params(),
        cost_estimate=pl.CostEstimate(flops=0, bytes_accessed=10 << 20, transcendentals=0),
        name="dense_tiles",
    )(codes, pltpu.with_memory_space_constraint(slab, pltpu.HBM))


def gather_kernel(member, dense, own, beside, beyond, bias, out):
    total = jnp.zeros((ROWS, WIDTH), F32)
    e = member[0]
    upper = e // 2
    for first, blocks in (
        (5 - e, own), (1 + 8 * upper - e, beside), (9 - 6 * upper - e, beyond)
    ):
        for i in range(blocks.shape[0]):
            total += jnp.dot(dense[first + i], blocks[i], preferred_element_type=F32)
    out[0:ROWS, :] = total.astype(BF16)
    out[ROWS:, :] = jnp.broadcast_to(bias[...], (16, WIDTH))


def gather_rows(member, dense, blocks, bias):
    return pl.pallas_call(
        gather_kernel,
        in_specs=[SMEM] + [VMEM] * 5,
        out_specs=VMEM,
        out_shape=jax.ShapeDtypeStruct((PACK_ROWS, WIDTH), BF16),
        compiler_params=params(),
        cost_estimate=pl.CostEstimate(
            flops=2 * OFFSETS * ROWS * ROWS * WIDTH, bytes_accessed=8 << 20, transcendentals=0
        ),
        name="aggregate_features",
    )(member, dense, *blocks, bias)


def middle_kernel(
    place, mixed, cots, weight, dense,
    act, part, ta, tb, tc, td, te,
    act_all, grad_all, feats,
):
    mine = pl.multiple_of(place[1] * WIDTH, WIDTH)
    bias = jnp.concatenate([mixed[c, ROWS:, :] for c in range(COLS)], axis=1)[0:1].astype(F32)
    step = 128
    for i in range(ROWS // step):
        span = slice(i * step, (i + 1) * step)
        rows = jnp.concatenate([mixed[c, span, :] for c in range(COLS)], axis=1)
        feats[span, :] = rows
        preact = jnp.dot(rows, weight[...], preferred_element_type=F32) + bias
        sig = 1.0 / (1.0 + jnp.exp(-preact))
        act_all[span, :] = (preact * sig).astype(BF16)
        cot = jnp.concatenate([cots[c, span, :] for c in range(COLS)], axis=1)
        grad_all[span, :] = (
            cot.astype(F32) * sig * (1.0 + preact * (1.0 - sig))
        ).astype(BF16)
    act[...] = act_all[:, pl.ds(mine, WIDTH)]
    grad_mine = grad_all[:, pl.ds(mine, WIDTH)].astype(F32)
    weight_grad = jnp.dot(
        grad_mine.T.astype(BF16), feats[...], preferred_element_type=F32
    )
    part[0:ROWS, :] = weight_grad.T
    first = lax.broadcasted_iota(jnp.int32, (RING * SHARE - HIDDEN, WIDTH), 0) == 0
    part[ROWS:, :] = jnp.where(first, jnp.sum(grad_mine, axis=0, keepdims=True), 0.0)
    back = lax.dot_general(
        weight[pl.ds(mine, WIDTH), :],
        grad_all[...],
        (((1,), (1,)), ((), ())),
        preferred_element_type=F32,
    ).astype(BF16)
    side = place[0] % 2
    for k, pair in enumerate((ta, tb, tc, td, te)):
        for s in range(2):
            pair[s] = jnp.dot(
                back, dense[2 * k + 1 + s - side], preferred_element_type=F32
            ).astype(BF16)


def middle(place, mixed, cots, weight, dense):
    return pl.pallas_call(
        middle_kernel,
        in_specs=[SMEM] + [VMEM] * 4,
        out_specs=[VMEM] * 7,
        out_shape=[
            jax.ShapeDtypeStruct((ROWS, WIDTH), BF16),
            jax.ShapeDtypeStruct((RING * SHARE, WIDTH), F32),
        ]
        + [jax.ShapeDtypeStruct((2, WIDTH, ROWS), BF16)] * 5,
        scratch_shapes=[pltpu.VMEM((ROWS, HIDDEN), BF16)] * 3,
        compiler_params=params(),
        cost_estimate=pl.CostEstimate(
            flops=2 * (OFFSETS + 9) * ROWS * ROWS * WIDTH, bytes_accessed=10 << 20, transcendentals=ROWS * HIDDEN
        ),
        name="activation_and_terms",
    )(place, mixed, cots, weight, dense)


def share_kernel(scale, shares, *rest):
    spread = rest[-1]
    total = jnp.sum(shares[...], axis=0) * scale
    spread[...] = jnp.broadcast_to(total.astype(spread.dtype)[None], spread.shape)


def spread_sum(shares, behind, copies, scale, dtype):
    return pl.pallas_call(
        lambda *refs: share_kernel(scale, *refs),
        in_specs=[VMEM] + [pl.BlockSpec(memory_space=pl.ANY)] * len(behind),
        out_specs=VMEM,
        out_shape=jax.ShapeDtypeStruct((copies, SHARE, WIDTH), dtype),
        compiler_params=params(),
        cost_estimate=pl.CostEstimate(flops=1 << 16, bytes_accessed=1 << 19, transcendentals=0),
        name="spread_sum",
    )(shares, *behind)


def split_kernel(side, own, ta, tb, td, te, first, keep, send):
    del first
    for s in range(2):
        total = own[s].astype(F32)
        for arrived in (ta, tb, td, te):
            total += arrived[s].astype(F32)

        @pl.when(side[0] == s)
        def _():
            keep[...] = total

        @pl.when(side[0] != s)
        def _():
            send[...] = total.astype(BF16)


def split_terms(side, own, arrived, first):
    return pl.pallas_call(
        split_kernel,
        in_specs=[SMEM] + [VMEM] * 5 + [pl.BlockSpec(memory_space=pl.ANY)],
        out_specs=[VMEM] * 2,
        out_shape=[
            jax.ShapeDtypeStruct((WIDTH, ROWS), F32),
            jax.ShapeDtypeStruct((WIDTH, ROWS), BF16),
        ],
        compiler_params=params(),
        cost_estimate=pl.CostEstimate(flops=1 << 20, bytes_accessed=2 << 20, transcendentals=0),
        name="pair_sums",
    )(side, own, *arrived, first)


def last_kernel(keep, arrived, first, out):
    del first
    out[...] = (keep[...] + arrived[...].astype(F32)).T.astype(BF16)


def last_sum(keep, arrived, first):
    return pl.pallas_call(
        last_kernel,
        in_specs=[VMEM] * 2 + [pl.BlockSpec(memory_space=pl.ANY)],
        out_specs=VMEM,
        out_shape=jax.ShapeDtypeStruct((ROWS, WIDTH), BF16),
        compiler_params=params(),
        cost_estimate=pl.CostEstimate(flops=1 << 17, bytes_accessed=1 << 19, transcendentals=0),
        name="node_gradient",
    )(keep, arrived, first)


def widen_kernel(whole, weight_grad, bias_grad):
    weight_grad[...] = whole[0:HIDDEN, :].astype(F32)
    bias_grad[...] = whole[HIDDEN : HIDDEN + 16, :].astype(F32)[0:1]


def widen(whole):
    return pl.pallas_call(
        widen_kernel,
        in_specs=[VMEM],
        out_specs=[VMEM] * 2,
        out_shape=[
            jax.ShapeDtypeStruct((HIDDEN, WIDTH), F32),
            jax.ShapeDtypeStruct((1, WIDTH), F32),
        ],
        compiler_params=params(),
        name="weight_gradient",
    )(whole)


def routed(block, source):
    route = []
    for p in range(PAIRS):
        for s in range(2):
            pair, other = source(p, s)
            route.append((2 * (pair % PAIRS) + other, 2 * p + s))
    return lax.ppermute(block, BLK, route)


def on_device(node_feats, weight, layer_bias, cotangent, adj_tiles, tile_row, tile_col, tile_count):
    member = lax.axis_index(FOUR).astype(jnp.int32).reshape(1)
    column = lax.axis_index(COL).astype(jnp.int32).reshape(1)
    slots = jnp.arange(SLOTS, dtype=jnp.int32)[None, :]
    dead = slots >= tile_count[0][:, None]
    codes = tile_row[0] * BLOCKS + tile_col[0] + BLOCKS * BLOCKS * dead.astype(jnp.int32)

    def one_away(block):
        return routed(block, lambda p, s: (p - 1 + 2 * (p % 2), s))

    with jax.named_scope("feature_halo"):
        four = lax.all_gather(node_feats, FOUR, axis=0, tiled=False)
        beside = one_away(four)
        pair = lax.dynamic_slice_in_dim(four, 2 * lax.axis_index("zp"), 2, 0)
        beyond = routed(pair, lambda p, s: (p + 2 - 4 * (p % 2), s))
    with jax.named_scope("column_gather"):
        cots = lax.all_gather(cotangent, COL, axis=0, tiled=False)
    dense = make_dense(codes, adj_tiles)
    mine = gather_rows(member, dense, (four, beside, beyond), layer_bias.reshape(1, WIDTH))
    with jax.named_scope("column_gather"):
        mixed = lax.all_gather(mine, COL, axis=0, tiled=False)
    act, part, ta, tb, tc, td, te = middle(
        jnp.concatenate([member, column]), mixed, cots, weight, dense
    )

    ring = ("zq", "zp", "xl")
    with jax.named_scope("weight_scatter"):
        shares = lax.all_to_all(part.reshape(RING, SHARE, WIDTH), ring, 0, 0, tiled=True)
    with jax.named_scope("term_halo"):
        ra, rb, rd, re = (
            routed(t, lambda p, s, k=k: (p - k, s)) for k, t in ((-2, ta), (-1, tb), (1, td), (2, te))
        )
    spread = spread_sum(shares, [rb], N_Y, 1.0, F32)
    with jax.named_scope("weight_rows"):
        shares = lax.all_to_all(spread, "y", 0, 0, tiled=True)
    keep, send = split_terms(lax.axis_index("xl").astype(jnp.int32).reshape(1), tc, (ra, rb, rd, re), spread)
    spread = spread_sum(shares, [keep], RING, float(NODES) ** -0.5, BF16)
    with jax.named_scope("term_exchange"):
        other = routed(send, lambda p, s: (p, 1 - s))
    grad_nodes = last_sum(keep, other, spread)
    with jax.named_scope("weight_gather"):
        whole = lax.all_to_all(spread, ring, 0, 0, tiled=True).reshape(RING * SHARE, WIDTH)
    weight_grad, bias_grad = widen(whole)
    return act, grad_nodes, weight_grad, bias_grad.reshape(WIDTH)


def solution(mesh):
    fine = Mesh(
        np.asarray(mesh.devices).reshape(N_Y, N_Z // 2, 2, N_XL, 2, 2), BLK + COL
    )
    placed = (
        P(BLK, COL),
        P(),
        P(COL),
        P(BLK, COL),
        P(BLK, None, None, None, None),
        P(BLK, None, None),
        P(BLK, None, None),
        P(BLK, None),
    )
    return jax.shard_map(
        on_device,
        mesh=fine,
        in_specs=placed,
        out_specs=(P(BLK, COL), P(BLK, COL), P(None, COL), P(COL)),
        check_vma=False,
    )
```

```python
import jax
import jax.numpy as jnp
import numpy as np
from jax import lax
from jax.experimental import pallas as pl
from jax.experimental.pallas import tpu as pltpu
from jax.sharding import Mesh
from jax.sharding import PartitionSpec as P

NODES = 98304
TILE = 128
BLOCKS = 4
ROWS = TILE * BLOCKS
WIDTH = 128
COLS = 4
HIDDEN = WIDTH * COLS
OFFSETS = 9
SLOTS = 16
REACH = 4
N_Y, N_Z, N_XL = 8, 12, 2
PAIRS = N_Y * N_Z
PACK_ROWS = ROWS + 16
RING = N_Z * N_XL
SHARE = 24
BLK = ("y", "z", "xl")
COL = ("xh", "core")
BF16 = jnp.bfloat16
F32 = jnp.float32
VMEM = pl.BlockSpec(memory_space=pltpu.VMEM)
SMEM = pl.BlockSpec(memory_space=pltpu.SMEM)


def params(mib=16):
    return pltpu.CompilerParams(vmem_limit_bytes=mib * 1024 * 1024)


def dense_kernel(codes, slab, dense, held, sems):
    copies = [
        pltpu.make_async_copy(slab.at[0, o], held.at[o], sems.at[o]) for o in range(OFFSETS)
    ]
    for copy in copies:
        copy.start()
    dense[0] = jnp.zeros((ROWS, ROWS), BF16)
    dense[OFFSETS + 1] = jnp.zeros((ROWS, ROWS), BF16)
    for offset, copy in enumerate(copies):
        copy.wait()
        for slot in range(SLOTS):
            code = codes[offset, slot]
            row = pl.multiple_of(((code >> 2) & 3) * TILE, TILE)
            col = pl.multiple_of((code & 3) * TILE, TILE)
            tile = held[offset, slot]
            dense[offset + 1, pl.ds(row, TILE), pl.ds(col, TILE)] = jnp.where(
                code < BLOCKS * BLOCKS, tile, jnp.zeros_like(tile)
            )


def make_dense(codes, slab):
    return pl.pallas_call(
        dense_kernel,
        in_specs=[SMEM, pl.BlockSpec(memory_space=pltpu.HBM)],
        out_specs=VMEM,
        out_shape=jax.ShapeDtypeStruct((OFFSETS + 2, ROWS, ROWS), BF16),
        scratch_shapes=[
            pltpu.VMEM((OFFSETS, SLOTS, TILE, TILE), BF16),
            pltpu.SemaphoreType.DMA((OFFSETS,)),
        ],
        compiler_params=params(),
        cost_estimate=pl.CostEstimate(flops=0, bytes_accessed=10 << 20, transcendentals=0),
        name="dense_tiles",
    )(codes, pltpu.with_memory_space_constraint(slab, pltpu.HBM))


def gather_kernel(side, dense, far_before, before, own, after, far_after, cross, bias, out):
    s = side[0]
    total = jnp.dot(dense[1], far_before[...], preferred_element_type=F32)
    total += jnp.dot(dense[9], far_after[...], preferred_element_type=F32)
    total += jnp.dot(dense[2 + 6 * s], cross[...], preferred_element_type=F32)
    for first, pair in ((3 - s, before), (5 - s, own), (7 - s, after)):
        for i in range(2):
            total += jnp.dot(dense[first + i], pair[i], preferred_element_type=F32)
    out[0:ROWS, :] = total.astype(BF16)
    out[ROWS:, :] = jnp.broadcast_to(bias[...], (16, WIDTH))


def gather_rows(side, dense, blocks, bias):
    return pl.pallas_call(
        gather_kernel,
        in_specs=[SMEM] + [VMEM] * 8,
        out_specs=VMEM,
        out_shape=jax.ShapeDtypeStruct((PACK_ROWS, WIDTH), BF16),
        compiler_params=params(),
        cost_estimate=pl.CostEstimate(
            flops=2 * OFFSETS * ROWS * ROWS * WIDTH, bytes_accessed=8 << 20, transcendentals=0
        ),
        name="aggregate_features",
    )(side, dense, *blocks, bias)


def middle_kernel(
    place, mixed, cots, weight, dense,
    act, part, ta, tb, tc, td, te,
    act_all, grad_all, feats,
):
    mine = pl.multiple_of(place[1] * WIDTH, WIDTH)
    bias = jnp.concatenate([mixed[c, ROWS:, :] for c in range(COLS)], axis=1)[0:1].astype(F32)
    step = 128
    for i in range(ROWS // step):
        span = slice(i * step, (i + 1) * step)
        rows = jnp.concatenate([mixed[c, span, :] for c in range(COLS)], axis=1)
        feats[span, :] = rows
        preact = jnp.dot(rows, weight[...], preferred_element_type=F32) + bias
        sig = 1.0 / (1.0 + jnp.exp(-preact))
        act_all[span, :] = (preact * sig).astype(BF16)
        cot = jnp.concatenate([cots[c, span, :] for c in range(COLS)], axis=1)
        grad_all[span, :] = (
            cot.astype(F32) * sig * (1.0 + preact * (1.0 - sig))
        ).astype(BF16)
    act[...] = act_all[:, pl.ds(mine, WIDTH)]
    grad_mine = grad_all[:, pl.ds(mine, WIDTH)].astype(F32)
    weight_grad = jnp.dot(
        grad_mine.T.astype(BF16), feats[...], preferred_element_type=F32
    )
    part[0:ROWS, :] = weight_grad.T
    first = lax.broadcasted_iota(jnp.int32, (RING * SHARE - HIDDEN, WIDTH), 0) == 0
    part[ROWS:, :] = jnp.where(first, jnp.sum(grad_mine, axis=0, keepdims=True), 0.0)
    back = lax.dot_general(
        weight[pl.ds(mine, WIDTH), :],
        grad_all[...],
        (((1,), (1,)), ((), ())),
        preferred_element_type=F32,
    ).astype(BF16)
    side = place[0]
    for k, pair in enumerate((ta, tb, tc, td, te)):
        for s in range(2):
            pair[s] = jnp.dot(
                back, dense[2 * k + 1 + s - side], preferred_element_type=F32
            ).astype(BF16)


def middle(place, mixed, cots, weight, dense):
    return pl.pallas_call(
        middle_kernel,
        in_specs=[SMEM] + [VMEM] * 4,
        out_specs=[VMEM] * 7,
        out_shape=[
            jax.ShapeDtypeStruct((ROWS, WIDTH), BF16),
            jax.ShapeDtypeStruct((RING * SHARE, WIDTH), F32),
        ]
        + [jax.ShapeDtypeStruct((2, WIDTH, ROWS), BF16)] * 5,
        scratch_shapes=[pltpu.VMEM((ROWS, HIDDEN), BF16)] * 3,
        compiler_params=params(),
        cost_estimate=pl.CostEstimate(
            flops=2 * (OFFSETS + 9) * ROWS * ROWS * WIDTH, bytes_accessed=10 << 20, transcendentals=ROWS * HIDDEN
        ),
        name="activation_and_terms",
    )(place, mixed, cots, weight, dense)


def share_kernel(scale, shares, *rest):
    spread = rest[-1]
    total = jnp.sum(shares[...], axis=0) * scale
    spread[...] = jnp.broadcast_to(total.astype(spread.dtype)[None], spread.shape)


def spread_sum(shares, behind, copies, scale, dtype):
    return pl.pallas_call(
        lambda *refs: share_kernel(scale, *refs),
        in_specs=[VMEM] + [pl.BlockSpec(memory_space=pl.ANY)] * len(behind),
        out_specs=VMEM,
        out_shape=jax.ShapeDtypeStruct((copies, SHARE, WIDTH), dtype),
        compiler_params=params(),
        cost_estimate=pl.CostEstimate(flops=1 << 16, bytes_accessed=1 << 19, transcendentals=0),
        name="spread_sum",
    )(shares, *behind)


def split_kernel(side, own, ta, tb, td, te, first, keep, send):
    del first
    for s in range(2):
        total = own[s].astype(F32)
        for arrived in (ta, tb, td, te):
            total += arrived[s].astype(F32)

        @pl.when(side[0] == s)
        def _():
            keep[...] = total

        @pl.when(side[0] != s)
        def _():
            send[...] = total.astype(BF16)


def split_terms(side, own, arrived, first):
    return pl.pallas_call(
        split_kernel,
        in_specs=[SMEM] + [VMEM] * 5 + [pl.BlockSpec(memory_space=pl.ANY)],
        out_specs=[VMEM] * 2,
        out_shape=[
            jax.ShapeDtypeStruct((WIDTH, ROWS), F32),
            jax.ShapeDtypeStruct((WIDTH, ROWS), BF16),
        ],
        compiler_params=params(),
        cost_estimate=pl.CostEstimate(flops=1 << 20, bytes_accessed=2 << 20, transcendentals=0),
        name="pair_sums",
    )(side, own, *arrived, first)


def last_kernel(keep, arrived, first, out):
    del first
    out[...] = (keep[...] + arrived[...].astype(F32)).T.astype(BF16)


def last_sum(keep, arrived, first):
    return pl.pallas_call(
        last_kernel,
        in_specs=[VMEM] * 2 + [pl.BlockSpec(memory_space=pl.ANY)],
        out_specs=VMEM,
        out_shape=jax.ShapeDtypeStruct((ROWS, WIDTH), BF16),
        compiler_params=params(),
        cost_estimate=pl.CostEstimate(flops=1 << 17, bytes_accessed=1 << 19, transcendentals=0),
        name="node_gradient",
    )(keep, arrived, first)


def widen_kernel(whole, weight_grad, bias_grad):
    weight_grad[...] = whole[0:HIDDEN, :].astype(F32)
    bias_grad[...] = whole[HIDDEN : HIDDEN + 16, :].astype(F32)[0:1]


def widen(whole):
    return pl.pallas_call(
        widen_kernel,
        in_specs=[VMEM],
        out_specs=[VMEM] * 2,
        out_shape=[
            jax.ShapeDtypeStruct((HIDDEN, WIDTH), F32),
            jax.ShapeDtypeStruct((1, WIDTH), F32),
        ],
        compiler_params=params(),
        name="weight_gradient",
    )(whole)


def routed(block, source):
    route = []
    for p in range(PAIRS):
        for s in range(2):
            pair, other = source(p, s)
            route.append((2 * (pair % PAIRS) + other, 2 * p + s))
    return lax.ppermute(block, BLK, route)


def on_device(node_feats, weight, layer_bias, cotangent, adj_tiles, tile_row, tile_col, tile_count):
    side = lax.axis_index("xl").astype(jnp.int32).reshape(1)
    column = lax.axis_index(COL).astype(jnp.int32).reshape(1)
    slots = jnp.arange(SLOTS, dtype=jnp.int32)[None, :]
    dead = slots >= tile_count[0][:, None]
    codes = tile_row[0] * BLOCKS + tile_col[0] + BLOCKS * BLOCKS * dead.astype(jnp.int32)

    with jax.named_scope("feature_halo"):
        x = node_feats
        far_before, far_after = (routed(x, lambda p, s, k=k: (p + k, s)) for k in (-2, 2))
        pair = lax.all_gather(x, "xl", axis=0, tiled=False)
        before, after = (routed(pair, lambda p, s, k=k: (p + k, s)) for k in (-1, 1))
        cross = jnp.where(side[0] == 1, far_before, far_after)
        cross = routed(cross, lambda p, s: (p, 1 - s))
    with jax.named_scope("column_gather"):
        cots = lax.all_gather(cotangent, COL, axis=0, tiled=False)
    dense = make_dense(codes, adj_tiles)
    blocks = (far_before, before, pair, after, far_after, cross)
    mine = gather_rows(side, dense, blocks, layer_bias.reshape(1, WIDTH))
    with jax.named_scope("column_gather"):
        mixed = lax.all_gather(mine, COL, axis=0, tiled=False)
    act, part, ta, tb, tc, td, te = middle(
        jnp.concatenate([side, column]), mixed, cots, weight, dense
    )

    ring = ("z", "xl")
    with jax.named_scope("weight_scatter"):
        shares = lax.all_to_all(part.reshape(RING, SHARE, WIDTH), ring, 0, 0, tiled=True)
    with jax.named_scope("term_halo"):
        ra, rb, rd, re = (
            routed(t, lambda p, s, k=k: (p - k, s)) for k, t in ((-2, ta), (-1, tb), (1, td), (2, te))
        )
    spread = spread_sum(shares, [rb], N_Y, 1.0, F32)
    with jax.named_scope("weight_rows"):
        shares = lax.all_to_all(spread, "y", 0, 0, tiled=True)
    keep, send = split_terms(side, tc, (ra, rb, rd, re), spread)
    spread = spread_sum(shares, [keep], RING, float(NODES) ** -0.5, BF16)
    with jax.named_scope("term_exchange"):
        other = routed(send, lambda p, s: (p, 1 - s))
    grad_nodes = last_sum(keep, other, spread)
    with jax.named_scope("weight_gather"):
        whole = lax.all_to_all(spread, ring, 0, 0, tiled=True).reshape(RING * SHARE, WIDTH)
    weight_grad, bias_grad = widen(whole)
    return act, grad_nodes, weight_grad, bias_grad.reshape(WIDTH)


def solution(mesh):
    fine = Mesh(
        np.asarray(mesh.devices).reshape(N_Y, N_Z, N_XL, 2, 2), BLK + COL
    )
    placed = (
        P(BLK, COL),
        P(),
        P(COL),
        P(BLK, COL),
        P(BLK, None, None, None, None),
        P(BLK, None, None),
        P(BLK, None, None),
        P(BLK, None),
    )
    return jax.shard_map(
        on_device,
        mesh=fine,
        in_specs=placed,
        out_specs=(P(BLK, COL), P(BLK, COL), P(None, COL), P(COL)),
        check_vma=False,
    )
```

```python
import jax
import jax.numpy as jnp
import numpy as np
from jax import lax
from jax.experimental import pallas as pl
from jax.experimental.pallas import tpu as pltpu
from jax.sharding import Mesh
from jax.sharding import PartitionSpec as P

NODES = 98304
TILE = 128
BLOCKS = 4
ROWS = TILE * BLOCKS
WIDTH = 128
COLS = 4
HIDDEN = WIDTH * COLS
OFFSETS = 9
SLOTS = 16
REACH = 4
N_Y, N_Z, N_XL = 8, 12, 2
PAIRS = N_Y * N_Z
RING = N_Z * N_XL
SHARE = 24
BLK = ("y", "z", "xl")
COL = ("xh", "core")
BF16 = jnp.bfloat16
F32 = jnp.float32
VMEM = pl.BlockSpec(memory_space=pltpu.VMEM)
SMEM = pl.BlockSpec(memory_space=pltpu.SMEM)


def params(mib=16):
    return pltpu.CompilerParams(vmem_limit_bytes=mib * 1024 * 1024)


def dense_kernel(codes, slab, dense, held, sems):
    copies = [
        pltpu.make_async_copy(slab.at[0, o], held.at[o], sems.at[o]) for o in range(OFFSETS)
    ]
    for copy in copies:
        copy.start()
    dense[0] = jnp.zeros((ROWS, ROWS), BF16)
    dense[OFFSETS + 1] = jnp.zeros((ROWS, ROWS), BF16)
    for offset, copy in enumerate(copies):
        copy.wait()
        for slot in range(SLOTS):
            code = codes[offset, slot]
            row = pl.multiple_of(((code >> 2) & 3) * TILE, TILE)
            col = pl.multiple_of((code & 3) * TILE, TILE)
            tile = held[offset, slot]
            dense[offset + 1, pl.ds(row, TILE), pl.ds(col, TILE)] = jnp.where(
                code < BLOCKS * BLOCKS, tile, jnp.zeros_like(tile)
            )


def make_dense(codes, slab):
    return pl.pallas_call(
        dense_kernel,
        in_specs=[SMEM, pl.BlockSpec(memory_space=pltpu.HBM)],
        out_specs=VMEM,
        out_shape=jax.ShapeDtypeStruct((OFFSETS + 2, ROWS, ROWS), BF16),
        scratch_shapes=[
            pltpu.VMEM((OFFSETS, SLOTS, TILE, TILE), BF16),
            pltpu.SemaphoreType.DMA((OFFSETS,)),
        ],
        compiler_params=params(),
        cost_estimate=pl.CostEstimate(flops=0, bytes_accessed=10 << 20, transcendentals=0),
        name="dense_tiles",
    )(codes, pltpu.with_memory_space_constraint(slab, pltpu.HBM))


def gather_kernel(side, dense, far_before, before, own, after, far_after, cross, out):
    s = side[0]
    total = jnp.dot(dense[1], far_before[...], preferred_element_type=F32)
    total += jnp.dot(dense[9], far_after[...], preferred_element_type=F32)
    total += jnp.dot(dense[2 + 6 * s], cross[...], preferred_element_type=F32)
    for first, pair in ((3 - s, before), (5 - s, own), (7 - s, after)):
        for i in range(2):
            total += jnp.dot(dense[first + i], pair[i], preferred_element_type=F32)
    out[...] = total.astype(BF16)


def gather_rows(side, dense, blocks):
    return pl.pallas_call(
        gather_kernel,
        in_specs=[SMEM] + [VMEM] * 7,
        out_specs=VMEM,
        out_shape=jax.ShapeDtypeStruct((ROWS, WIDTH), BF16),
        compiler_params=params(),
        cost_estimate=pl.CostEstimate(
            flops=2 * OFFSETS * ROWS * ROWS * WIDTH, bytes_accessed=8 << 20, transcendentals=0
        ),
        name="aggregate_features",
    )(side, dense, *blocks)


def middle_kernel(
    place, mixed, cot, bias, weight, dense,
    act, part, ta, tb, tc, td, te,
    grad, feats,
):
    mine = pl.multiple_of(place[1] * WIDTH, WIDTH)
    columns = weight[:, pl.ds(mine, WIDTH)]
    step = 128
    for i in range(ROWS // step):
        span = slice(i * step, (i + 1) * step)
        rows = jnp.concatenate([mixed[c, span, :] for c in range(COLS)], axis=1)
        feats[span, :] = rows
        preact = jnp.dot(rows, columns, preferred_element_type=F32) + bias[...].astype(F32)
        sig = 1.0 / (1.0 + jnp.exp(-preact))
        act[span, :] = (preact * sig).astype(BF16)
        grad[span, :] = (
            cot[span, :].astype(F32) * sig * (1.0 + preact * (1.0 - sig))
        ).astype(BF16)
    grad_mine = grad[...].astype(F32)
    back = grad_mine.T.astype(BF16)
    weight_grad = jnp.dot(back, feats[...], preferred_element_type=F32)
    part[0:ROWS, :] = weight_grad.T
    first = lax.broadcasted_iota(jnp.int32, (RING * SHARE - HIDDEN, WIDTH), 0) == 0
    part[ROWS:, :] = jnp.where(first, jnp.sum(grad_mine, axis=0, keepdims=True), 0.0)
    side = place[0]
    for k, pair in enumerate((ta, tb, tc, td, te)):
        for s in range(2):
            pair[s] = jnp.dot(
                back, dense[2 * k + 1 + s - side], preferred_element_type=F32
            ).astype(BF16)


def middle(place, mixed, cot, bias, weight, dense):
    return pl.pallas_call(
        middle_kernel,
        in_specs=[SMEM] + [VMEM] * 5,
        out_specs=[VMEM] * 7,
        out_shape=[
            jax.ShapeDtypeStruct((ROWS, WIDTH), BF16),
            jax.ShapeDtypeStruct((RING * SHARE, WIDTH), F32),
        ]
        + [jax.ShapeDtypeStruct((2, WIDTH, ROWS), BF16)] * 5,
        scratch_shapes=[pltpu.VMEM((ROWS, WIDTH), BF16), pltpu.VMEM((ROWS, HIDDEN), BF16)],
        compiler_params=params(),
        cost_estimate=pl.CostEstimate(
            flops=2 * (OFFSETS + 9) * ROWS * ROWS * WIDTH, bytes_accessed=10 << 20, transcendentals=ROWS * WIDTH
        ),
        name="activation_and_terms",
    )(place, mixed, cot, bias, weight, dense)


def share_kernel(scale, shares, *rest):
    spread = rest[-1]
    total = jnp.sum(shares[...], axis=0) * scale
    spread[...] = jnp.broadcast_to(total.astype(spread.dtype)[None], spread.shape)


def spread_sum(shares, behind, copies, scale, dtype):
    return pl.pallas_call(
        lambda *refs: share_kernel(scale, *refs),
        in_specs=[VMEM] + [pl.BlockSpec(memory_space=pl.ANY)] * len(behind),
        out_specs=VMEM,
        out_shape=jax.ShapeDtypeStruct((copies, SHARE, WIDTH), dtype),
        compiler_params=params(),
        cost_estimate=pl.CostEstimate(flops=1 << 16, bytes_accessed=1 << 19, transcendentals=0),
        name="spread_sum",
    )(shares, *behind)


def split_kernel(side, own, ta, tb, td, te, first, keep, send):
    del first
    for s in range(2):
        total = own[s].astype(F32)
        for arrived in (ta, tb, td, te):
            total += arrived[s].astype(F32)

        @pl.when(side[0] == s)
        def _():
            keep[...] = total

        @pl.when(side[0] != s)
        def _():
            send[...] = total.astype(BF16)


def split_terms(side, own, arrived, first):
    return pl.pallas_call(
        split_kernel,
        in_specs=[SMEM] + [VMEM] * 5 + [pl.BlockSpec(memory_space=pl.ANY)],
        out_specs=[VMEM] * 2,
        out_shape=[
            jax.ShapeDtypeStruct((WIDTH, ROWS), F32),
            jax.ShapeDtypeStruct((WIDTH, ROWS), BF16),
        ],
        compiler_params=params(),
        cost_estimate=pl.CostEstimate(flops=1 << 20, bytes_accessed=2 << 20, transcendentals=0),
        name="pair_sums",
    )(side, own, *arrived, first)


def last_kernel(keep, arrived, first, out):
    del first
    out[...] = (keep[...] + arrived[...].astype(F32)).T.astype(BF16)


def last_sum(keep, arrived, first):
    return pl.pallas_call(
        last_kernel,
        in_specs=[VMEM] * 2 + [pl.BlockSpec(memory_space=pl.ANY)],
        out_specs=VMEM,
        out_shape=jax.ShapeDtypeStruct((ROWS, WIDTH), BF16),
        compiler_params=params(),
        cost_estimate=pl.CostEstimate(flops=1 << 17, bytes_accessed=1 << 19, transcendentals=0),
        name="projected_gradient",
    )(keep, arrived, first)


def node_kernel(column, grads, weight, out):
    mine = pl.multiple_of(column[0] * WIDTH, WIDTH)
    rows = jnp.concatenate([grads[c] for c in range(COLS)], axis=1)
    out[...] = lax.dot_general(
        rows,
        weight[pl.ds(mine, WIDTH), :],
        (((1,), (1,)), ((), ())),
        preferred_element_type=F32,
    ).astype(BF16)


def node_gradient(column, grads, weight):
    return pl.pallas_call(
        node_kernel,
        in_specs=[SMEM] + [VMEM] * 2,
        out_specs=VMEM,
        out_shape=jax.ShapeDtypeStruct((ROWS, WIDTH), BF16),
        compiler_params=params(),
        cost_estimate=pl.CostEstimate(
            flops=2 * ROWS * HIDDEN * WIDTH, bytes_accessed=2 << 20, transcendentals=0
        ),
        name="node_gradient",
    )(column, grads, weight)


def widen_kernel(whole, weight_grad, bias_grad):
    weight_grad[...] = whole[0:HIDDEN, :].astype(F32)
    bias_grad[...] = whole[HIDDEN : HIDDEN + 16, :].astype(F32)[0:1]


def widen(whole):
    return pl.pallas_call(
        widen_kernel,
        in_specs=[VMEM],
        out_specs=[VMEM] * 2,
        out_shape=[
            jax.ShapeDtypeStruct((HIDDEN, WIDTH), F32),
            jax.ShapeDtypeStruct((1, WIDTH), F32),
        ],
        compiler_params=params(),
        name="weight_gradient",
    )(whole)


def routed(block, source):
    route = []
    for p in range(PAIRS):
        for s in range(2):
            pair, other = source(p, s)
            route.append((2 * (pair % PAIRS) + other, 2 * p + s))
    return lax.ppermute(block, BLK, route)


def on_device(node_feats, weight, layer_bias, cotangent, adj_tiles, tile_row, tile_col, tile_count):
    side = lax.axis_index("xl").astype(jnp.int32).reshape(1)
    column = lax.axis_index(COL).astype(jnp.int32).reshape(1)
    slots = jnp.arange(SLOTS, dtype=jnp.int32)[None, :]
    dead = slots >= tile_count[0][:, None]
    codes = tile_row[0] * BLOCKS + tile_col[0] + BLOCKS * BLOCKS * dead.astype(jnp.int32)

    with jax.named_scope("feature_halo"):
        x = node_feats
        far_before, far_after = (routed(x, lambda p, s, k=k: (p + k, s)) for k in (-2, 2))
        pair = lax.all_gather(x, "xl", axis=0, tiled=False)
        before, after = (routed(pair, lambda p, s, k=k: (p + k, s)) for k in (-1, 1))
        cross = jnp.where(side[0] == 1, far_before, far_after)
        cross = routed(cross, lambda p, s: (p, 1 - s))
    dense = make_dense(codes, adj_tiles)
    blocks = (far_before, before, pair, after, far_after, cross)
    mine = gather_rows(side, dense, blocks)
    with jax.named_scope("column_gather"):
        mixed = lax.all_gather(mine, COL, axis=0, tiled=False)
    act, part, ta, tb, tc, td, te = middle(
        jnp.concatenate([side, column]), mixed, cotangent, layer_bias.reshape(1, WIDTH), weight, dense
    )

    ring = ("z", "xl")
    with jax.named_scope("weight_scatter"):
        shares = lax.all_to_all(part.reshape(RING, SHARE, WIDTH), ring, 0, 0, tiled=True)
    with jax.named_scope("term_halo"):
        ra, rb, rd, re = (
            routed(t, lambda p, s, k=k: (p - k, s)) for k, t in ((-2, ta), (-1, tb), (1, td), (2, te))
        )
    spread = spread_sum(shares, [rb], N_Y, 1.0, F32)
    with jax.named_scope("weight_rows"):
        shares = lax.all_to_all(spread, "y", 0, 0, tiled=True)
    keep, send = split_terms(side, tc, (ra, rb, rd, re), spread)
    with jax.named_scope("term_exchange"):
        other = routed(send, lambda p, s: (p, 1 - s))
    spread = spread_sum(shares, [other], RING, float(NODES) ** -0.5, BF16)
    grad_proj = last_sum(keep, other, spread)
    with jax.named_scope("column_gather"):
        grads = lax.all_gather(grad_proj, COL, axis=0, tiled=False)
    grad_nodes = node_gradient(column, grads, weight)
    with jax.named_scope("weight_gather"):
        whole = lax.all_to_all(spread, ring, 0, 0, tiled=True).reshape(RING * SHARE, WIDTH)
    weight_grad, bias_grad = widen(whole)
    return act, grad_nodes, weight_grad, bias_grad.reshape(WIDTH)


def solution(mesh):
    fine = Mesh(
        np.asarray(mesh.devices).reshape(N_Y, N_Z, N_XL, 2, 2), BLK + COL
    )
    placed = (
        P(BLK, COL),
        P(),
        P(COL),
        P(BLK, COL),
        P(BLK, None, None, None, None),
        P(BLK, None, None),
        P(BLK, None, None),
        P(BLK, None),
    )
    return jax.shard_map(
        on_device,
        mesh=fine,
        in_specs=placed,
        out_specs=(P(BLK, COL), P(BLK, COL), P(None, COL), P(COL)),
        check_vma=False,
    )
```

```python
import jax
import jax.numpy as jnp
import numpy as np
from jax import lax
from jax.experimental import pallas as pl
from jax.experimental.pallas import tpu as pltpu
from jax.sharding import Mesh
from jax.sharding import PartitionSpec as P

NODES = 98304
TILE = 128
BLOCKS = 4
ROWS = TILE * BLOCKS
WIDTH = 128
COLS = 4
HIDDEN = WIDTH * COLS
OFFSETS = 9
SLOTS = 16
REACH = 4
N_Y, N_Z, N_XL = 8, 12, 2
PAIRS = N_Y * N_Z
RING = N_Z * N_XL
SHARE = 24
BLK = ("y", "z", "xl")
COL = ("xh", "core")
BF16 = jnp.bfloat16
F32 = jnp.float32
VMEM = pl.BlockSpec(memory_space=pltpu.VMEM)
SMEM = pl.BlockSpec(memory_space=pltpu.SMEM)


def params(mib=16):
    return pltpu.CompilerParams(vmem_limit_bytes=mib * 1024 * 1024)


def dense_kernel(codes, slab, dense, held, sems):
    copies = [
        pltpu.make_async_copy(slab.at[0, o], held.at[o], sems.at[o]) for o in range(OFFSETS)
    ]
    for copy in copies:
        copy.start()
    for offset, copy in enumerate(copies):
        copy.wait()
        for slot in range(SLOTS):
            code = codes[offset, slot]
            row = pl.multiple_of(((code >> 2) & 3) * TILE, TILE)
            col = pl.multiple_of((code & 3) * TILE, TILE)
            tile = held[offset, slot]
            dense[offset, pl.ds(row, TILE), pl.ds(col, TILE)] = jnp.where(
                code < BLOCKS * BLOCKS, tile, jnp.zeros_like(tile)
            )


def make_dense(codes, slab):
    return pl.pallas_call(
        dense_kernel,
        in_specs=[SMEM, pl.BlockSpec(memory_space=pltpu.HBM)],
        out_specs=VMEM,
        out_shape=jax.ShapeDtypeStruct((OFFSETS, ROWS, ROWS), BF16),
        scratch_shapes=[
            pltpu.VMEM((OFFSETS, SLOTS, TILE, TILE), BF16),
            pltpu.SemaphoreType.DMA((OFFSETS,)),
        ],
        compiler_params=params(),
        cost_estimate=pl.CostEstimate(flops=0, bytes_accessed=10 << 20, transcendentals=0),
        name="dense_tiles",
    )(codes, pltpu.with_memory_space_constraint(slab, pltpu.HBM))


def gather_kernel(side, dense, far_before, before, own, after, far_after, cross, out):
    s = side[0]
    total = jnp.dot(dense[0], far_before[...], preferred_element_type=F32)
    total += jnp.dot(dense[8], far_after[...], preferred_element_type=F32)
    total += jnp.dot(dense[1 + 6 * s], cross[...], preferred_element_type=F32)
    for first, pair in ((2 - s, before), (4 - s, own), (6 - s, after)):
        for i in range(2):
            total += jnp.dot(dense[first + i], pair[i], preferred_element_type=F32)
    out[...] = total.astype(BF16)


def gather_rows(side, dense, blocks):
    return pl.pallas_call(
        gather_kernel,
        in_specs=[SMEM] + [VMEM] * 7,
        out_specs=VMEM,
        out_shape=jax.ShapeDtypeStruct((ROWS, WIDTH), BF16),
        compiler_params=params(),
        cost_estimate=pl.CostEstimate(
            flops=2 * OFFSETS * ROWS * ROWS * WIDTH, bytes_accessed=8 << 20, transcendentals=0
        ),
        name="aggregate_features",
    )(side, dense, *blocks)


def middle_kernel(
    place, mixed, cot, bias, weight, dense,
    act, part, cross, tb, tc, td, ta, te,
    grad, feats,
):
    mine = pl.multiple_of(place[1] * WIDTH, WIDTH)
    columns = weight[:, pl.ds(mine, WIDTH)]
    step = 128
    for i in range(ROWS // step):
        span = slice(i * step, (i + 1) * step)
        rows = jnp.concatenate([mixed[c, span, :] for c in range(COLS)], axis=1)
        feats[span, :] = rows
        preact = jnp.dot(rows, columns, preferred_element_type=F32) + bias[...].astype(F32)
        sig = 1.0 / (1.0 + jnp.exp(-preact))
        act[span, :] = (preact * sig).astype(BF16)
        grad[span, :] = (
            cot[span, :].astype(F32) * sig * (1.0 + preact * (1.0 - sig))
        ).astype(BF16)
    grad_mine = grad[...].astype(F32)
    back = grad_mine.T.astype(BF16)
    weight_grad = jnp.dot(back, feats[...], preferred_element_type=F32)
    part[0:ROWS, :] = weight_grad.T
    first = lax.broadcasted_iota(jnp.int32, (RING * SHARE - HIDDEN, WIDTH), 0) == 0
    part[ROWS:, :] = jnp.where(first, jnp.sum(grad_mine, axis=0, keepdims=True), 0.0)
    side = place[0]
    for k, term in ((1 + 6 * side, cross), (0, ta), (8, te)):
        term[...] = jnp.dot(back, dense[k], preferred_element_type=F32).astype(BF16)
    for first, pair in ((2 - side, tb), (4 - side, tc), (6 - side, td)):
        for i in range(2):
            pair[i] = jnp.dot(back, dense[first + i], preferred_element_type=F32).astype(BF16)


def middle(place, mixed, cot, bias, weight, dense):
    return pl.pallas_call(
        middle_kernel,
        in_specs=[SMEM] + [VMEM] * 5,
        out_specs=[VMEM] * 8,
        out_shape=[
            jax.ShapeDtypeStruct((ROWS, WIDTH), BF16),
            jax.ShapeDtypeStruct((RING * SHARE, WIDTH), F32),
        ]
        + [jax.ShapeDtypeStruct((WIDTH, ROWS), BF16)]
        + [jax.ShapeDtypeStruct((2, WIDTH, ROWS), BF16)] * 3
        + [jax.ShapeDtypeStruct((WIDTH, ROWS), BF16)] * 2,
        scratch_shapes=[pltpu.VMEM((ROWS, WIDTH), BF16), pltpu.VMEM((ROWS, HIDDEN), BF16)],
        compiler_params=params(),
        cost_estimate=pl.CostEstimate(
            flops=2 * (OFFSETS + 9) * ROWS * ROWS * WIDTH, bytes_accessed=10 << 20, transcendentals=ROWS * WIDTH
        ),
        name="activation_and_terms",
    )(place, mixed, cot, bias, weight, dense)


def share_kernel(scale, shares, *rest):
    spread = rest[-1]
    total = jnp.sum(shares[...], axis=0) * scale
    spread[...] = jnp.broadcast_to(total.astype(spread.dtype)[None], spread.shape)


def spread_sum(shares, behind, copies, scale, dtype):
    return pl.pallas_call(
        lambda *refs: share_kernel(scale, *refs),
        in_specs=[VMEM] + [pl.BlockSpec(memory_space=pl.ANY)] * len(behind),
        out_specs=VMEM,
        out_shape=jax.ShapeDtypeStruct((copies, SHARE, WIDTH), dtype),
        compiler_params=params(),
        cost_estimate=pl.CostEstimate(flops=1 << 16, bytes_accessed=1 << 19, transcendentals=0),
        name="spread_sum",
    )(shares, *behind)


def far_kernel(side, ta, te, cross, out_a, out_e):
    r = cross[...].astype(F32)
    out_a[...] = (ta[...].astype(F32) + jnp.where(side[0] == 1, r, 0.0)).astype(BF16)
    out_e[...] = (te[...].astype(F32) + jnp.where(side[0] == 0, r, 0.0)).astype(BF16)


def far_sums(side, ta, te, cross):
    return pl.pallas_call(
        far_kernel,
        in_specs=[SMEM] + [VMEM] * 3,
        out_specs=[VMEM] * 2,
        out_shape=[jax.ShapeDtypeStruct((WIDTH, ROWS), BF16)] * 2,
        compiler_params=params(),
        cost_estimate=pl.CostEstimate(flops=1 << 18, bytes_accessed=1 << 20, transcendentals=0),
        name="far_sums",
    )(side, ta, te, cross)


def split_kernel(side, own, tb, td, ta, te, first, keep, send):
    del first
    for s in range(2):
        total = own[s].astype(F32) + tb[s].astype(F32) + td[s].astype(F32)

        @pl.when(side[0] == s)
        def _():
            keep[...] = total + ta[...].astype(F32) + te[...].astype(F32)

        @pl.when(side[0] != s)
        def _():
            send[...] = total.astype(BF16)


def split_terms(side, own, arrived, first):
    return pl.pallas_call(
        split_kernel,
        in_specs=[SMEM] + [VMEM] * 5 + [pl.BlockSpec(memory_space=pl.ANY)],
        out_specs=[VMEM] * 2,
        out_shape=[
            jax.ShapeDtypeStruct((WIDTH, ROWS), F32),
            jax.ShapeDtypeStruct((WIDTH, ROWS), BF16),
        ],
        compiler_params=params(),
        cost_estimate=pl.CostEstimate(flops=1 << 20, bytes_accessed=2 << 20, transcendentals=0),
        name="pair_sums",
    )(side, own, *arrived, first)


def last_kernel(keep, arrived, first, out):
    del first
    out[...] = (keep[...] + arrived[...].astype(F32)).T.astype(BF16)


def last_sum(keep, arrived, first):
    return pl.pallas_call(
        last_kernel,
        in_specs=[VMEM] * 2 + [pl.BlockSpec(memory_space=pl.ANY)],
        out_specs=VMEM,
        out_shape=jax.ShapeDtypeStruct((ROWS, WIDTH), BF16),
        compiler_params=params(),
        cost_estimate=pl.CostEstimate(flops=1 << 17, bytes_accessed=1 << 19, transcendentals=0),
        name="projected_gradient",
    )(keep, arrived, first)


def node_kernel(column, grads, weight, out):
    mine = pl.multiple_of(column[0] * WIDTH, WIDTH)
    rows = jnp.concatenate([grads[c] for c in range(COLS)], axis=1)
    out[...] = lax.dot_general(
        rows,
        weight[pl.ds(mine, WIDTH), :],
        (((1,), (1,)), ((), ())),
        preferred_element_type=F32,
    ).astype(BF16)


def node_gradient(column, grads, weight):
    return pl.pallas_call(
        node_kernel,
        in_specs=[SMEM] + [VMEM] * 2,
        out_specs=VMEM,
        out_shape=jax.ShapeDtypeStruct((ROWS, WIDTH), BF16),
        compiler_params=params(),
        cost_estimate=pl.CostEstimate(
            flops=2 * ROWS * HIDDEN * WIDTH, bytes_accessed=2 << 20, transcendentals=0
        ),
        name="node_gradient",
    )(column, grads, weight)


def widen_kernel(whole, weight_grad, bias_grad):
    weight_grad[...] = whole[0:HIDDEN, :].astype(F32)
    bias_grad[...] = whole[HIDDEN : HIDDEN + 16, :].astype(F32)[0:1]


def widen(whole):
    return pl.pallas_call(
        widen_kernel,
        in_specs=[VMEM],
        out_specs=[VMEM] * 2,
        out_shape=[
            jax.ShapeDtypeStruct((HIDDEN, WIDTH), F32),
            jax.ShapeDtypeStruct((1, WIDTH), F32),
        ],
        compiler_params=params(),
        name="weight_gradient",
    )(whole)


def routed(block, source):
    route = []
    for p in range(PAIRS):
        for s in range(2):
            pair, other = source(p, s)
            route.append((2 * (pair % PAIRS) + other, 2 * p + s))
    return lax.ppermute(block, BLK, route)


def on_device(node_feats, weight, layer_bias, cotangent, adj_tiles, tile_row, tile_col, tile_count):
    side = lax.axis_index("xl").astype(jnp.int32).reshape(1)
    column = lax.axis_index(COL).astype(jnp.int32).reshape(1)
    slots = jnp.arange(SLOTS, dtype=jnp.int32)[None, :]
    dead = slots >= tile_count[0][:, None]
    codes = tile_row[0] * BLOCKS + tile_col[0] + BLOCKS * BLOCKS * dead.astype(jnp.int32)

    with jax.named_scope("feature_halo"):
        x = node_feats
        far_before, far_after = (routed(x, lambda p, s, k=k: (p + k, s)) for k in (-2, 2))
        pair = lax.all_gather(x, "xl", axis=0, tiled=False)
        before, after = (routed(pair, lambda p, s, k=k: (p + k, s)) for k in (-1, 1))
        cross = jnp.where(side[0] == 1, far_before, far_after)
        cross = routed(cross, lambda p, s: (p, 1 - s))
    dense = make_dense(codes, adj_tiles)
    blocks = (far_before, before, pair, after, far_after, cross)
    mine = gather_rows(side, dense, blocks)
    with jax.named_scope("column_gather"):
        mixed = lax.all_gather(mine, COL, axis=0, tiled=False)
    act, part, cross, tb, tc, td, ta, te = middle(
        jnp.concatenate([side, column]), mixed, cotangent, layer_bias.reshape(1, WIDTH), weight, dense
    )

    ring = ("z", "xl")
    with jax.named_scope("weight_scatter"):
        shares = lax.all_to_all(part.reshape(RING, SHARE, WIDTH), ring, 0, 0, tiled=True)
    with jax.named_scope("term_halo"):
        cross = routed(cross, lambda p, s: (p, 1 - s))
        rb, rd = (routed(t, lambda p, s, k=k: (p - k, s)) for k, t in ((-1, tb), (1, td)))
        ta, te = far_sums(side, ta, te, cross)
        ra, re = (routed(t, lambda p, s, k=k: (p - k, s)) for k, t in ((-2, ta), (2, te)))
    spread = spread_sum(shares, [ta], N_Y, 1.0, F32)
    with jax.named_scope("weight_rows"):
        shares = lax.all_to_all(spread, "y", 0, 0, tiled=True)
    keep, send = split_terms(side, tc, (rb, rd, ra, re), spread)
    with jax.named_scope("term_exchange"):
        other = routed(send, lambda p, s: (p, 1 - s))
    spread = spread_sum(shares, [other], RING, float(NODES) ** -0.5, BF16)
    grad_proj = last_sum(keep, other, spread)
    with jax.named_scope("column_gather"):
        grads = lax.all_gather(grad_proj, COL, axis=0, tiled=False)
    grad_nodes = node_gradient(column, grads, weight)
    with jax.named_scope("weight_gather"):
        whole = lax.all_to_all(spread, ring, 0, 0, tiled=True).reshape(RING * SHARE, WIDTH)
    weight_grad, bias_grad = widen(whole)
    return act, grad_nodes, weight_grad, bias_grad.reshape(WIDTH)


def solution(mesh):
    fine = Mesh(
        np.asarray(mesh.devices).reshape(N_Y, N_Z, N_XL, 2, 2), BLK + COL
    )
    placed = (
        P(BLK, COL),
        P(),
        P(COL),
        P(BLK, COL),
        P(BLK, None, None, None, None),
        P(BLK, None, None),
        P(BLK, None, None),
        P(BLK, None),
    )
    return jax.shard_map(
        on_device,
        mesh=fine,
        in_specs=placed,
        out_specs=(P(BLK, COL), P(BLK, COL), P(None, COL), P(COL)),
        check_vma=False,
    )
```

```python
import jax
import jax.numpy as jnp
import numpy as np
from jax import lax
from jax.experimental import pallas as pl
from jax.experimental.pallas import tpu as pltpu
from jax.sharding import Mesh
from jax.sharding import PartitionSpec as P

NODES = 98304
TILE = 128
BLOCKS = 4
ROWS = TILE * BLOCKS
WIDTH = 128
COLS = 4
HIDDEN = WIDTH * COLS
OFFSETS = 9
SLOTS = 16
REACH = 4
N_Y, N_Z, N_XL = 8, 12, 2
PAIRS = N_Y * N_Z
RING = N_Z * N_XL
SHARE = 24
BLK = ("y", "z", "xl")
COL = ("xh", "core")
BF16 = jnp.bfloat16
F32 = jnp.float32
VMEM = pl.BlockSpec(memory_space=pltpu.VMEM)
SMEM = pl.BlockSpec(memory_space=pltpu.SMEM)


def params(mib=16):
    return pltpu.CompilerParams(vmem_limit_bytes=mib * 1024 * 1024)


def dense_kernel(codes, slab, dense, held, sems):
    copies = [
        pltpu.make_async_copy(slab.at[0, o], held.at[o], sems.at[o]) for o in range(OFFSETS)
    ]
    for copy in copies:
        copy.start()
    for offset, copy in enumerate(copies):
        copy.wait()
        for slot in range(SLOTS):
            code = codes[offset, slot]
            row = pl.multiple_of(((code >> 2) & 3) * TILE, TILE)
            col = pl.multiple_of((code & 3) * TILE, TILE)
            tile = held[offset, slot]
            dense[offset, pl.ds(row, TILE), pl.ds(col, TILE)] = jnp.where(
                code < BLOCKS * BLOCKS, tile, jnp.zeros_like(tile)
            )


def make_dense(codes, slab):
    return pl.pallas_call(
        dense_kernel,
        in_specs=[SMEM, pl.BlockSpec(memory_space=pltpu.HBM)],
        out_specs=VMEM,
        out_shape=jax.ShapeDtypeStruct((OFFSETS, ROWS, ROWS), BF16),
        scratch_shapes=[
            pltpu.VMEM((OFFSETS, SLOTS, TILE, TILE), BF16),
            pltpu.SemaphoreType.DMA((OFFSETS,)),
        ],
        compiler_params=params(),
        cost_estimate=pl.CostEstimate(flops=0, bytes_accessed=10 << 20, transcendentals=0),
        name="dense_tiles",
    )(codes, pltpu.with_memory_space_constraint(slab, pltpu.HBM))


def pair_kernel(side, x, other, out):
    out[side[0]] = x[...]
    out[1 - side[0]] = other[...]


def make_pair(side, x, other):
    return pl.pallas_call(
        pair_kernel,
        in_specs=[SMEM] + [VMEM] * 2,
        out_specs=VMEM,
        out_shape=jax.ShapeDtypeStruct((2, ROWS, WIDTH), BF16),
        compiler_params=params(),
        cost_estimate=pl.CostEstimate(flops=0, bytes_accessed=1 << 19, transcendentals=0),
        name="pair_blocks",
    )(side, x, other)


def gather_kernel(side, dense, far_before, before, own, after, far_after, cross, out):
    s = side[0]
    total = jnp.dot(dense[0], far_before[...], preferred_element_type=F32)
    total += jnp.dot(dense[8], far_after[...], preferred_element_type=F32)
    total += jnp.dot(dense[1 + 6 * s], cross[...], preferred_element_type=F32)
    for first, pair in ((2 - s, before), (4 - s, own), (6 - s, after)):
        for i in range(2):
            total += jnp.dot(dense[first + i], pair[i], preferred_element_type=F32)
    out[...] = total.astype(BF16)


def gather_rows(side, dense, blocks):
    return pl.pallas_call(
        gather_kernel,
        in_specs=[SMEM] + [VMEM] * 7,
        out_specs=VMEM,
        out_shape=jax.ShapeDtypeStruct((ROWS, WIDTH), BF16),
        compiler_params=params(),
        cost_estimate=pl.CostEstimate(
            flops=2 * OFFSETS * ROWS * ROWS * WIDTH, bytes_accessed=8 << 20, transcendentals=0
        ),
        name="aggregate_features",
    )(side, dense, *blocks)


def middle_kernel(
    place, mixed, cot, bias, weight, dense,
    act, part, cross, tb, tc, td, ta, te,
    grad, feats,
):
    mine = pl.multiple_of(place[1] * WIDTH, WIDTH)
    columns = weight[:, pl.ds(mine, WIDTH)]
    step = 128
    for i in range(ROWS // step):
        span = slice(i * step, (i + 1) * step)
        rows = jnp.concatenate([mixed[c, span, :] for c in range(COLS)], axis=1)
        feats[span, :] = rows
        preact = jnp.dot(rows, columns, preferred_element_type=F32) + bias[...].astype(F32)
        sig = 1.0 / (1.0 + jnp.exp(-preact))
        act[span, :] = (preact * sig).astype(BF16)
        grad[span, :] = (
            cot[span, :].astype(F32) * sig * (1.0 + preact * (1.0 - sig))
        ).astype(BF16)
    grad_mine = grad[...].astype(F32)
    back = grad_mine.T.astype(BF16)
    weight_grad = jnp.dot(back, feats[...], preferred_element_type=F32)
    part[0:ROWS, :] = weight_grad.T
    first = lax.broadcasted_iota(jnp.int32, (RING * SHARE - HIDDEN, WIDTH), 0) == 0
    part[ROWS:, :] = jnp.where(first, jnp.sum(grad_mine, axis=0, keepdims=True), 0.0)
    side = place[0]
    for k, term in ((1 + 6 * side, cross), (0, ta), (8, te)):
        term[...] = jnp.dot(back, dense[k], preferred_element_type=F32).astype(BF16)
    for first, pair in ((2 - side, tb), (4 - side, tc), (6 - side, td)):
        for i in range(2):
            pair[i] = jnp.dot(back, dense[first + i], preferred_element_type=F32).astype(BF16)


def middle(place, mixed, cot, bias, weight, dense):
    return pl.pallas_call(
        middle_kernel,
        in_specs=[SMEM] + [VMEM] * 5,
        out_specs=[VMEM] * 8,
        out_shape=[
            jax.ShapeDtypeStruct((ROWS, WIDTH), BF16),
            jax.ShapeDtypeStruct((RING * SHARE, WIDTH), F32),
        ]
        + [jax.ShapeDtypeStruct((WIDTH, ROWS), BF16)]
        + [jax.ShapeDtypeStruct((2, WIDTH, ROWS), BF16)] * 3
        + [jax.ShapeDtypeStruct((WIDTH, ROWS), BF16)] * 2,
        scratch_shapes=[pltpu.VMEM((ROWS, WIDTH), BF16), pltpu.VMEM((ROWS, HIDDEN), BF16)],
        compiler_params=params(),
        cost_estimate=pl.CostEstimate(
            flops=2 * (OFFSETS + 9) * ROWS * ROWS * WIDTH, bytes_accessed=10 << 20, transcendentals=ROWS * WIDTH
        ),
        name="activation_and_terms",
    )(place, mixed, cot, bias, weight, dense)


def share_kernel(scale, shares, *rest):
    spread = rest[-1]
    total = jnp.sum(shares[...], axis=0) * scale
    spread[...] = jnp.broadcast_to(total.astype(spread.dtype)[None], spread.shape)


def spread_sum(shares, behind, copies, scale, dtype):
    return pl.pallas_call(
        lambda *refs: share_kernel(scale, *refs),
        in_specs=[VMEM] + [pl.BlockSpec(memory_space=pl.ANY)] * len(behind),
        out_specs=VMEM,
        out_shape=jax.ShapeDtypeStruct((copies, SHARE, WIDTH), dtype),
        compiler_params=params(),
        cost_estimate=pl.CostEstimate(flops=1 << 16, bytes_accessed=1 << 19, transcendentals=0),
        name="spread_sum",
    )(shares, *behind)


def far_kernel(side, ta, te, cross, out_a, out_e):
    r = cross[...].astype(F32)
    out_a[...] = (ta[...].astype(F32) + jnp.where(side[0] == 1, r, 0.0)).astype(BF16)
    out_e[...] = (te[...].astype(F32) + jnp.where(side[0] == 0, r, 0.0)).astype(BF16)


def far_sums(side, ta, te, cross):
    return pl.pallas_call(
        far_kernel,
        in_specs=[SMEM] + [VMEM] * 3,
        out_specs=[VMEM] * 2,
        out_shape=[jax.ShapeDtypeStruct((WIDTH, ROWS), BF16)] * 2,
        compiler_params=params(),
        cost_estimate=pl.CostEstimate(flops=1 << 18, bytes_accessed=1 << 20, transcendentals=0),
        name="far_sums",
    )(side, ta, te, cross)


def split_kernel(side, own, tb, td, ta, te, first, keep, send):
    del first
    for s in range(2):
        total = own[s].astype(F32) + tb[s].astype(F32) + td[s].astype(F32)

        @pl.when(side[0] == s)
        def _():
            keep[...] = total + ta[...].astype(F32) + te[...].astype(F32)

        @pl.when(side[0] != s)
        def _():
            send[...] = total.astype(BF16)


def split_terms(side, own, arrived, first):
    return pl.pallas_call(
        split_kernel,
        in_specs=[SMEM] + [VMEM] * 5 + [pl.BlockSpec(memory_space=pl.ANY)],
        out_specs=[VMEM] * 2,
        out_shape=[
            jax.ShapeDtypeStruct((WIDTH, ROWS), F32),
            jax.ShapeDtypeStruct((WIDTH, ROWS), BF16),
        ],
        compiler_params=params(),
        cost_estimate=pl.CostEstimate(flops=1 << 20, bytes_accessed=2 << 20, transcendentals=0),
        name="pair_sums",
    )(side, own, *arrived, first)


def last_kernel(keep, arrived, shares, out, spread):
    out[...] = (keep[...] + arrived[...].astype(F32)).T.astype(BF16)
    share_kernel(float(NODES) ** -0.5, shares, spread)


def last_sum(keep, arrived, shares):
    return pl.pallas_call(
        last_kernel,
        in_specs=[VMEM] * 3,
        out_specs=[VMEM] * 2,
        out_shape=[
            jax.ShapeDtypeStruct((ROWS, WIDTH), BF16),
            jax.ShapeDtypeStruct((RING, SHARE, WIDTH), BF16),
        ],
        compiler_params=params(),
        cost_estimate=pl.CostEstimate(flops=1 << 17, bytes_accessed=1 << 19, transcendentals=0),
        name="projected_gradient",
    )(keep, arrived, shares)


def final_kernel(column, grads, weight, whole, nodes, weight_grad, bias_grad):
    mine = pl.multiple_of(column[0] * WIDTH, WIDTH)
    rows = jnp.concatenate([grads[c] for c in range(COLS)], axis=1)
    nodes[...] = lax.dot_general(
        rows,
        weight[pl.ds(mine, WIDTH), :],
        (((1,), (1,)), ((), ())),
        preferred_element_type=F32,
    ).astype(BF16)
    weight_grad[...] = whole[0:HIDDEN, :].astype(F32)
    bias_grad[...] = whole[HIDDEN : HIDDEN + 16, :].astype(F32)[0:1]


def final(column, grads, weight, whole):
    return pl.pallas_call(
        final_kernel,
        in_specs=[SMEM] + [VMEM] * 3,
        out_specs=[VMEM] * 3,
        out_shape=[
            jax.ShapeDtypeStruct((ROWS, WIDTH), BF16),
            jax.ShapeDtypeStruct((HIDDEN, WIDTH), F32),
            jax.ShapeDtypeStruct((1, WIDTH), F32),
        ],
        compiler_params=params(),
        cost_estimate=pl.CostEstimate(
            flops=2 * ROWS * HIDDEN * WIDTH, bytes_accessed=2 << 20, transcendentals=0
        ),
        name="gradients",
    )(column, grads, weight, whole)


def routed(block, source):
    route = []
    for p in range(PAIRS):
        for s in range(2):
            pair, other = source(p, s)
            route.append((2 * (pair % PAIRS) + other, 2 * p + s))
    return lax.ppermute(block, BLK, route)


def on_device(node_feats, weight, layer_bias, cotangent, adj_tiles, tile_row, tile_col, tile_count):
    side = lax.axis_index("xl").astype(jnp.int32).reshape(1)
    column = lax.axis_index(COL).astype(jnp.int32).reshape(1)
    slots = jnp.arange(SLOTS, dtype=jnp.int32)[None, :]
    dead = slots >= tile_count[0][:, None]
    codes = tile_row[0] * BLOCKS + tile_col[0] + BLOCKS * BLOCKS * dead.astype(jnp.int32)

    with jax.named_scope("feature_halo"):
        x = node_feats
        far_before, far_after = (routed(x, lambda p, s, k=k: (p + k, s)) for k in (-2, 2))
        pair = make_pair(side, x, routed(x, lambda p, s: (p, 1 - s)))
        before, after = (routed(pair, lambda p, s, k=k: (p + k, s)) for k in (-1, 1))
        cross = jnp.where(side[0] == 1, far_before, far_after)
        cross = routed(cross, lambda p, s: (p, 1 - s))
    dense = make_dense(codes, adj_tiles)
    blocks = (far_before, before, pair, after, far_after, cross)
    mine = gather_rows(side, dense, blocks)
    with jax.named_scope("column_gather"):
        mixed = lax.all_gather(mine, COL, axis=0, tiled=False)
    act, part, cross, tb, tc, td, ta, te = middle(
        jnp.concatenate([side, column]), mixed, cotangent, layer_bias.reshape(1, WIDTH), weight, dense
    )

    ring = ("z", "xl")
    with jax.named_scope("weight_scatter"):
        shares = lax.all_to_all(part.reshape(RING, SHARE, WIDTH), ring, 0, 0, tiled=True)
    with jax.named_scope("term_halo"):
        cross = routed(cross, lambda p, s: (p, 1 - s))
        rb, rd = (routed(t, lambda p, s, k=k: (p - k, s)) for k, t in ((-1, tb), (1, td)))
        ta, te = far_sums(side, ta, te, cross)
        ra, re = (routed(t, lambda p, s, k=k: (p - k, s)) for k, t in ((-2, ta), (2, te)))
    spread = spread_sum(shares, [ta], N_Y, 1.0, F32)
    with jax.named_scope("weight_rows"):
        shares = lax.all_to_all(spread, "y", 0, 0, tiled=True)
    keep, send = split_terms(side, tc, (rb, rd, ra, re), spread)
    with jax.named_scope("term_exchange"):
        other = routed(send, lambda p, s: (p, 1 - s))
    grad_proj, spread = last_sum(keep, other, shares)
    with jax.named_scope("weight_gather"):
        whole = lax.all_to_all(spread, ring, 0, 0, tiled=True).reshape(RING * SHARE, WIDTH)
    with jax.named_scope("column_gather"):
        grads = lax.all_gather(grad_proj, COL, axis=0, tiled=False)
    grad_nodes, weight_grad, bias_grad = final(column, grads, weight, whole)
    return act, grad_nodes, weight_grad, bias_grad.reshape(WIDTH)


def solution(mesh):
    fine = Mesh(
        np.asarray(mesh.devices).reshape(N_Y, N_Z, N_XL, 2, 2), BLK + COL
    )
    placed = (
        P(BLK, COL),
        P(),
        P(COL),
        P(BLK, COL),
        P(BLK, None, None, None, None),
        P(BLK, None, None),
        P(BLK, None, None),
        P(BLK, None),
    )
    return jax.shard_map(
        on_device,
        mesh=fine,
        in_specs=placed,
        out_specs=(P(BLK, COL), P(BLK, COL), P(None, COL), P(COL)),
        check_vma=False,
    )
```

```python
import jax
import jax.numpy as jnp
import numpy as np
from jax import lax
from jax.experimental import pallas as pl
from jax.experimental.pallas import tpu as pltpu
from jax.sharding import Mesh
from jax.sharding import PartitionSpec as P

NODES = 98304
TILE = 128
BLOCKS = 4
ROWS = TILE * BLOCKS
WIDTH = 128
COLS = 4
HIDDEN = WIDTH * COLS
OFFSETS = 9
SLOTS = 16
REACH = 4
N_Y, N_Z, N_XL = 8, 12, 2
PAIRS = N_Y * N_Z
RING = N_Z * N_XL
SHARE = 24
BLK = ("y", "z", "xl")
COL = ("xh", "core")
BF16 = jnp.bfloat16
F32 = jnp.float32
VMEM = pl.BlockSpec(memory_space=pltpu.VMEM)
SMEM = pl.BlockSpec(memory_space=pltpu.SMEM)


def params(mib=16):
    return pltpu.CompilerParams(vmem_limit_bytes=mib * 1024 * 1024)


def dense_kernel(codes, slab, dense, held, sems):
    copies = [
        pltpu.make_async_copy(slab.at[0, o], held.at[o], sems.at[o]) for o in range(OFFSETS)
    ]
    for copy in copies:
        copy.start()
    for offset, copy in enumerate(copies):
        copy.wait()
        for slot in range(SLOTS):
            code = codes[offset, slot]
            row = pl.multiple_of(((code >> 2) & 3) * TILE, TILE)
            col = pl.multiple_of((code & 3) * TILE, TILE)
            tile = held[offset, slot]
            dense[offset, pl.ds(row, TILE), pl.ds(col, TILE)] = jnp.where(
                code < BLOCKS * BLOCKS, tile, jnp.zeros_like(tile)
            )


def make_dense(codes, slab):
    return pl.pallas_call(
        dense_kernel,
        in_specs=[SMEM, pl.BlockSpec(memory_space=pltpu.HBM)],
        out_specs=VMEM,
        out_shape=jax.ShapeDtypeStruct((OFFSETS, ROWS, ROWS), BF16),
        scratch_shapes=[
            pltpu.VMEM((OFFSETS, SLOTS, TILE, TILE), BF16),
            pltpu.SemaphoreType.DMA((OFFSETS,)),
        ],
        compiler_params=params(),
        cost_estimate=pl.CostEstimate(flops=0, bytes_accessed=10 << 20, transcendentals=0),
        name="dense_tiles",
    )(codes, pltpu.with_memory_space_constraint(slab, pltpu.HBM))


def pair_kernel(side, x, other, out, sem):
    copy = pltpu.make_async_copy(x, out.at[side[0]], sem)
    copy.start()
    out[1 - side[0]] = other[...]
    copy.wait()


def make_pair(side, x, other):
    return pl.pallas_call(
        pair_kernel,
        in_specs=[SMEM, pl.BlockSpec(memory_space=pltpu.HBM), VMEM],
        out_specs=VMEM,
        out_shape=jax.ShapeDtypeStruct((2, ROWS, WIDTH), BF16),
        scratch_shapes=[pltpu.SemaphoreType.DMA],
        compiler_params=params(),
        cost_estimate=pl.CostEstimate(flops=0, bytes_accessed=1 << 19, transcendentals=0),
        name="pair_blocks",
    )(side, pltpu.with_memory_space_constraint(x, pltpu.HBM), other)


def gather_kernel(side, dense, far_before, before, own, after, far_after, cross, out):
    s = side[0]
    total = jnp.dot(dense[0], far_before[...], preferred_element_type=F32)
    total += jnp.dot(dense[8], far_after[...], preferred_element_type=F32)
    total += jnp.dot(dense[1 + 6 * s], cross[...], preferred_element_type=F32)
    for first, pair in ((2 - s, before), (4 - s, own), (6 - s, after)):
        for i in range(2):
            total += jnp.dot(dense[first + i], pair[i], preferred_element_type=F32)
    out[...] = total.astype(BF16)


def gather_rows(side, dense, blocks):
    return pl.pallas_call(
        gather_kernel,
        in_specs=[SMEM] + [VMEM] * 7,
        out_specs=VMEM,
        out_shape=jax.ShapeDtypeStruct((ROWS, WIDTH), BF16),
        compiler_params=params(),
        cost_estimate=pl.CostEstimate(
            flops=2 * OFFSETS * ROWS * ROWS * WIDTH, bytes_accessed=8 << 20, transcendentals=0
        ),
        name="aggregate_features",
    )(side, dense, *blocks)


def middle_kernel(
    place, mixed, cot, bias, weight, dense,
    act, part, cross, tb, tc, td, ta, te,
    grad, feats,
):
    mine = pl.multiple_of(place[1] * WIDTH, WIDTH)
    columns = weight[:, pl.ds(mine, WIDTH)]
    step = 128
    for i in range(ROWS // step):
        span = slice(i * step, (i + 1) * step)
        rows = jnp.concatenate([mixed[c, span, :] for c in range(COLS)], axis=1)
        feats[span, :] = rows
        preact = jnp.dot(rows, columns, preferred_element_type=F32) + bias[...].astype(F32)
        sig = 1.0 / (1.0 + jnp.exp(-preact))
        act[span, :] = (preact * sig).astype(BF16)
        grad[span, :] = (
            cot[span, :].astype(F32) * sig * (1.0 + preact * (1.0 - sig))
        ).astype(BF16)
    grad_mine = grad[...].astype(F32)
    back = grad_mine.T.astype(BF16)
    weight_grad = jnp.dot(back, feats[...], preferred_element_type=F32)
    part[0:ROWS, :] = weight_grad.T
    first = lax.broadcasted_iota(jnp.int32, (RING * SHARE - HIDDEN, WIDTH), 0) == 0
    part[ROWS:, :] = jnp.where(first, jnp.sum(grad_mine, axis=0, keepdims=True), 0.0)
    side = place[0]
    for k, term in ((1 + 6 * side, cross), (0, ta), (8, te)):
        term[...] = jnp.dot(back, dense[k], preferred_element_type=F32).astype(BF16)
    for first, pair in ((2 - side, tb), (4 - side, tc), (6 - side, td)):
        for i in range(2):
            pair[i] = jnp.dot(back, dense[first + i], preferred_element_type=F32).astype(BF16)


def middle(place, mixed, cot, bias, weight, dense):
    return pl.pallas_call(
        middle_kernel,
        in_specs=[SMEM] + [VMEM] * 5,
        out_specs=[VMEM] * 8,
        out_shape=[
            jax.ShapeDtypeStruct((ROWS, WIDTH), BF16),
            jax.ShapeDtypeStruct((RING * SHARE, WIDTH), F32),
        ]
        + [jax.ShapeDtypeStruct((WIDTH, ROWS), BF16)]
        + [jax.ShapeDtypeStruct((2, WIDTH, ROWS), BF16)] * 3
        + [jax.ShapeDtypeStruct((WIDTH, ROWS), BF16)] * 2,
        scratch_shapes=[pltpu.VMEM((ROWS, WIDTH), BF16), pltpu.VMEM((ROWS, HIDDEN), BF16)],
        compiler_params=params(),
        cost_estimate=pl.CostEstimate(
            flops=2 * (OFFSETS + 9) * ROWS * ROWS * WIDTH, bytes_accessed=10 << 20, transcendentals=ROWS * WIDTH
        ),
        name="activation_and_terms",
    )(place, mixed, cot, bias, weight, dense)


def share_kernel(scale, shares, *rest):
    spread = rest[-1]
    total = jnp.sum(shares[...], axis=0) * scale
    spread[...] = jnp.broadcast_to(total.astype(spread.dtype)[None], spread.shape)


def spread_sum(shares, behind, copies, scale, dtype):
    return pl.pallas_call(
        lambda *refs: share_kernel(scale, *refs),
        in_specs=[VMEM] + [pl.BlockSpec(memory_space=pl.ANY)] * len(behind),
        out_specs=VMEM,
        out_shape=jax.ShapeDtypeStruct((copies, SHARE, WIDTH), dtype),
        compiler_params=params(),
        cost_estimate=pl.CostEstimate(flops=1 << 16, bytes_accessed=1 << 19, transcendentals=0),
        name="spread_sum",
    )(shares, *behind)


def far_kernel(side, ta, te, cross, out_a, out_e):
    r = cross[...].astype(F32)
    out_a[...] = (ta[...].astype(F32) + jnp.where(side[0] == 1, r, 0.0)).astype(BF16)
    out_e[...] = (te[...].astype(F32) + jnp.where(side[0] == 0, r, 0.0)).astype(BF16)


def far_sums(side, ta, te, cross):
    return pl.pallas_call(
        far_kernel,
        in_specs=[SMEM] + [VMEM] * 3,
        out_specs=[VMEM] * 2,
        out_shape=[jax.ShapeDtypeStruct((WIDTH, ROWS), BF16)] * 2,
        compiler_params=params(),
        cost_estimate=pl.CostEstimate(flops=1 << 18, bytes_accessed=1 << 20, transcendentals=0),
        name="far_sums",
    )(side, ta, te, cross)


def split_kernel(side, own, tb, td, ta, te, first, keep, send):
    del first
    for s in range(2):
        total = own[s].astype(F32) + tb[s].astype(F32) + td[s].astype(F32)

        @pl.when(side[0] == s)
        def _():
            keep[...] = total + ta[...].astype(F32) + te[...].astype(F32)

        @pl.when(side[0] != s)
        def _():
            send[...] = total.astype(BF16)


def split_terms(side, own, arrived, first):
    return pl.pallas_call(
        split_kernel,
        in_specs=[SMEM] + [VMEM] * 5 + [pl.BlockSpec(memory_space=pl.ANY)],
        out_specs=[VMEM] * 2,
        out_shape=[
            jax.ShapeDtypeStruct((WIDTH, ROWS), F32),
            jax.ShapeDtypeStruct((WIDTH, ROWS), BF16),
        ],
        compiler_params=params(),
        cost_estimate=pl.CostEstimate(flops=1 << 20, bytes_accessed=2 << 20, transcendentals=0),
        name="pair_sums",
    )(side, own, *arrived, first)


def last_kernel(keep, arrived, shares, out, spread):
    out[...] = (keep[...] + arrived[...].astype(F32)).T.astype(BF16)
    share_kernel(float(NODES) ** -0.5, shares, spread)


def last_sum(keep, arrived, shares):
    return pl.pallas_call(
        last_kernel,
        in_specs=[VMEM] * 3,
        out_specs=[VMEM] * 2,
        out_shape=[
            jax.ShapeDtypeStruct((ROWS, WIDTH), BF16),
            jax.ShapeDtypeStruct((RING, SHARE, WIDTH), BF16),
        ],
        compiler_params=params(),
        cost_estimate=pl.CostEstimate(flops=1 << 17, bytes_accessed=1 << 19, transcendentals=0),
        name="projected_gradient",
    )(keep, arrived, shares)


def final_kernel(column, grads, weight, whole, nodes, weight_grad, bias_grad):
    mine = pl.multiple_of(column[0] * WIDTH, WIDTH)
    rows = jnp.concatenate([grads[c] for c in range(COLS)], axis=1)
    nodes[...] = lax.dot_general(
        rows,
        weight[pl.ds(mine, WIDTH), :],
        (((1,), (1,)), ((), ())),
        preferred_element_type=F32,
    ).astype(BF16)
    weight_grad[...] = whole[0:HIDDEN, :].astype(F32)
    bias_grad[...] = whole[HIDDEN : HIDDEN + 16, :].astype(F32)[0:1]


def final(column, grads, weight, whole):
    return pl.pallas_call(
        final_kernel,
        in_specs=[SMEM] + [VMEM] * 3,
        out_specs=[VMEM] * 3,
        out_shape=[
            jax.ShapeDtypeStruct((ROWS, WIDTH), BF16),
            jax.ShapeDtypeStruct((HIDDEN, WIDTH), F32),
            jax.ShapeDtypeStruct((1, WIDTH), F32),
        ],
        compiler_params=params(),
        cost_estimate=pl.CostEstimate(
            flops=2 * ROWS * HIDDEN * WIDTH, bytes_accessed=2 << 20, transcendentals=0
        ),
        name="gradients",
    )(column, grads, weight, whole)


def routed(block, source):
    route = []
    for p in range(PAIRS):
        for s in range(2):
            pair, other = source(p, s)
            route.append((2 * (pair % PAIRS) + other, 2 * p + s))
    return lax.ppermute(block, BLK, route)


def on_device(node_feats, weight, layer_bias, cotangent, adj_tiles, tile_row, tile_col, tile_count):
    side = lax.axis_index("xl").astype(jnp.int32).reshape(1)
    column = lax.axis_index(COL).astype(jnp.int32).reshape(1)
    slots = jnp.arange(SLOTS, dtype=jnp.int32)[None, :]
    dead = slots >= tile_count[0][:, None]
    codes = tile_row[0] * BLOCKS + tile_col[0] + BLOCKS * BLOCKS * dead.astype(jnp.int32)

    with jax.named_scope("feature_halo"):
        x = node_feats
        far_before, far_after = (routed(x, lambda p, s, k=k: (p + k, s)) for k in (-2, 2))
        pair = make_pair(side, x, routed(x, lambda p, s: (p, 1 - s)))
        before, after = (routed(pair, lambda p, s, k=k: (p + k, s)) for k in (-1, 1))
        cross = jnp.where(side[0] == 1, far_before, far_after)
        cross = routed(cross, lambda p, s: (p, 1 - s))
    dense = make_dense(codes, adj_tiles)
    blocks = (far_before, before, pair, after, far_after, cross)
    mine = gather_rows(side, dense, blocks)
    with jax.named_scope("column_gather"):
        mixed = lax.all_gather(mine, COL, axis=0, tiled=False)
    act, part, cross, tb, tc, td, ta, te = middle(
        jnp.concatenate([side, column]), mixed, cotangent, layer_bias.reshape(1, WIDTH), weight, dense
    )

    ring = ("z", "xl")
    with jax.named_scope("weight_scatter"):
        shares = lax.all_to_all(part.reshape(RING, SHARE, WIDTH), ring, 0, 0, tiled=True)
    with jax.named_scope("term_halo"):
        cross = routed(cross, lambda p, s: (p, 1 - s))
        rb, rd = (routed(t, lambda p, s, k=k: (p - k, s)) for k, t in ((-1, tb), (1, td)))
        ta, te = far_sums(side, ta, te, cross)
        ra, re = (routed(t, lambda p, s, k=k: (p - k, s)) for k, t in ((-2, ta), (2, te)))
    spread = spread_sum(shares, [ta], N_Y, 1.0, F32)
    with jax.named_scope("weight_rows"):
        shares = lax.all_to_all(spread, "y", 0, 0, tiled=True)
    keep, send = split_terms(side, tc, (rb, rd, ra, re), spread)
    with jax.named_scope("term_exchange"):
        other = routed(send, lambda p, s: (p, 1 - s))
    grad_proj, spread = last_sum(keep, other, shares)
    with jax.named_scope("weight_gather"):
        whole = lax.all_to_all(spread, ring, 0, 0, tiled=True).reshape(RING * SHARE, WIDTH)
    with jax.named_scope("column_gather"):
        grads = lax.all_gather(grad_proj, COL, axis=0, tiled=False)
    grad_nodes, weight_grad, bias_grad = final(column, grads, weight, whole)
    return act, grad_nodes, weight_grad, bias_grad.reshape(WIDTH)


def solution(mesh):
    fine = Mesh(
        np.asarray(mesh.devices).reshape(N_Y, N_Z, N_XL, 2, 2), BLK + COL
    )
    placed = (
        P(BLK, COL),
        P(),
        P(COL),
        P(BLK, COL),
        P(BLK, None, None, None, None),
        P(BLK, None, None),
        P(BLK, None, None),
        P(BLK, None),
    )
    return jax.shard_map(
        on_device,
        mesh=fine,
        in_specs=placed,
        out_specs=(P(BLK, COL), P(BLK, COL), P(None, COL), P(COL)),
        check_vma=False,
    )
```
